128 devices in a mesh: expert: 32 (over x, y, core), dp: 4 (over z).
Axes of the slice: x: 4, y: 4, z: 4, core: 2. Of those that a mesh axis runs over, the one named last changes fastest.
Arguments:
- tokens: bfloat16 [32768, 2048], P(('expert', 'dp')), may hold values from -6 to 6
- grad_out: bfloat16 [32768, 2048], P(('expert', 'dp')), may hold values from -6 to 6
- routes: int32 [32768, 2], P(('expert', 'dp')), may hold values from 0 to 31, all different within a row; in each aligned block of 256 rows (0 to 255, 256 to 511, ...) at most 32 rows name the same one
- gate_probs: bfloat16 [32768, 2], P(('expert', 'dp')), may hold values from 0.099609375 to 1
- w_gate: bfloat16 [32, 768, 2048], P('expert'), may hold values from -0.125 to 0.125
- w_up: bfloat16 [32, 768, 2048], P('expert'), may hold values from -0.125 to 0.125
- w_down: bfloat16 [32, 768, 2048], P('expert'), may hold values from -0.21875 to 0.21875
Outputs:
- d_tokens: bfloat16 [32768, 2048], P(('expert', 'dp'))
- d_probs: float32 [32768, 2], P(('expert', 'dp'))
- grad_w_gate: float32 [32, 768, 2048], P('expert', 'dp')
- grad_w_up: float32 [32, 768, 2048], P('expert', 'dp')
- grad_w_down: float32 [32, 768, 2048], P('expert', 'dp')
The draws below stay inside these ranges and needn't reach their ends.
Inputs may be any that keep to these rules, and one draw needn't show every extreme that they name: `routes`: within the 256 rows of one device (aligned blocks), each expert is named at most 32 times, a bound that some block reaches; the two experts of a row differ.
All inputs are finite; a program needn't handle non-finite values.
Results may differ from the reference program's by a relative error of at most 0.0049.
Values may be sent and summed in bfloat16 or wider, within the bound.
A program may use at most 192 MiB of HBM per device.

```python
import math
import jax
import jax.numpy as jnp
import numpy as np
from jax import lax

D = 2048
FF = 768
TOK_DEV = 256
EXPERTS = 32
CAP = 32
TOKENS = 32768
N_EXPERT = 32
N_DP = 4


def shard_levels(stream_key, shape, pieces, low, high):
    def one(position, blocks):
        steps = jax.random.uniform(jax.random.fold_in(jax.random.fold_in(stream_key, 6), position), (blocks,), jnp.float32, low / len(pieces), high / len(pieces))
        return jnp.repeat(jnp.exp(steps), shape[position] // blocks).reshape((-1,) + (1,) * (len(shape) - position - 1))

    gain = one(*pieces[0])
    for cut in pieces[1:]:
        gain = gain * one(*cut)
    return gain


def deal_out(key, own, number, rows, count, top, limit, skew):
    order = jax.random.permutation(key, count)
    crowded, ordinary = shares(count, rows * top, limit, skew, True), shares(count, rows * top, limit, skew, False)
    places = jnp.arange(count)

    def named(sizes, rotation):
        used = int((sizes > 0).sum())
        fixed = max(1, used // 4)
        passed = fixed + (places - fixed + rotation * (used - fixed)) % max(1, count - fixed)
        return jnp.zeros((count,), jnp.int32).at[order[jnp.where(places < fixed, places, passed)]].set(jnp.asarray(sizes, jnp.int32))

    sizes = jnp.where(number % 4 == 0, named(crowded, number // 4), named(ordinary, number - number // 4 - 1))
    mixed = jax.random.permutation(jax.random.fold_in(own, 3), count)
    source_of, taker = mixed[0:count // 2 * 2:2], mixed[1:count // 2 * 2:2]
    margin = jnp.minimum(sizes[source_of] - 1, limit - sizes[taker]) // 2
    margin = jnp.where((source_of == order[0]) | (taker == order[0]) | (sizes[taker] == 0), 0, jnp.maximum(margin, 0))
    passed = jax.random.randint(jax.random.fold_in(own, 4), (count // 2,), 0, 1 << 20) % (margin + 1)
    sizes = sizes.at[source_of].add(-passed).at[taker].add(passed)
    labels = jnp.searchsorted(jnp.cumsum(sizes), jnp.arange(rows * top), side="right").astype(jnp.int32)
    grid = labels.reshape(top, rows).T
    grid = grid[jax.random.permutation(jax.random.fold_in(own, 1), rows)]
    rotation = jax.random.randint(jax.random.fold_in(own, 2), (rows, 1), 0, top)
    return jnp.take_along_axis(grid, (jnp.arange(top)[None, :] + rotation) % top, axis=1)


def shares(number_of, total, bound, lean, full):
    weights = [(1 << 20) // math.isqrt(grade ** lean) + 1 for grade in range(1, number_of + 1)]
    largest = bound if full else min(bound, max(-(-total // number_of), total * weights[0] // sum(weights)))
    least = 1 if total - largest >= number_of - 1 else 0
    holding, rest = [largest] + [least] * (number_of - 1), total - largest - least * (number_of - 1)
    while rest > 0:
        candidates = [i for i in range(1, number_of) if holding[i] < largest] or [i for i in range(1, number_of) if holding[i] < bound]
        mass, budget = sum([weights[i] for i in candidates]), rest
        for i in candidates:
            more = min(bound - holding[i], max(1, budget * weights[i] // mass), rest)
            holding[i] = holding[i] + more
            rest = rest - more
    return np.array(holding)


def gaussian(key, extent, spread, reach, pieces=(), kind=jnp.bfloat16):
    result = jax.random.normal(key, extent, jnp.float32) * spread
    if len(pieces) > 0:
        result = shard_levels(key, extent, pieces, -0.22, 0.18) * result
    return jnp.clip(result, min=-reach, max=reach).astype(kind)


def setup_inputs(seed: int = 0) -> dict:
    streams_of = jax.random.split(jax.random.key(seed), 8)
    tokens = gaussian(streams_of[0], (TOKENS, D), 1.0, 6.0, ((0, 128),))
    grad_out = gaussian(streams_of[1], (TOKENS, D), 1.0, 6.0, ((0, 128),))
    routes_keys = jax.random.split(jax.random.fold_in(streams_of[2], 1), TOKENS // TOK_DEV)
    routes_turns = jax.random.permutation(jax.random.fold_in(streams_of[2], 3), TOKENS // TOK_DEV)
    routes = jax.vmap(lambda own, number: deal_out(jax.random.fold_in(streams_of[2], 2), own, number, TOK_DEV, EXPERTS, 2, CAP, 2))(routes_keys, routes_turns).reshape((TOKENS, 2))
    gate_probs = jnp.clip(0.099609375 + 0.9003906 * jax.random.uniform(streams_of[3], (TOKENS, 2), jnp.float32) ** shard_levels(streams_of[3], (TOKENS, 2), ((0, 128),), -0.2, 0.2), 0.099609375, 1.0).astype(jnp.bfloat16)
    w_gate = gaussian(streams_of[4], (EXPERTS, FF, D), D ** -0.5, 0.125, ((0, 32),))
    w_up = gaussian(streams_of[5], (EXPERTS, FF, D), D ** -0.5, 0.125, ((0, 32),))
    w_down = gaussian(streams_of[6], (EXPERTS, FF, D), FF ** -0.5, 0.21875, ((0, 32),))
    return dict(tokens=tokens, grad_out=grad_out, routes=routes, gate_probs=gate_probs, w_gate=w_gate, w_up=w_up, w_down=w_down)


def forward_part(x_rows, dy_rows, p_rows, w_g, w_u, w_d):
    contract_d = (((1,), (1,)), ((), ()))
    gate_pre = lax.dot_general(x_rows, w_g, contract_d, preferred_element_type=jnp.float32)
    upward = lax.dot_general(x_rows, w_u, contract_d, preferred_element_type=jnp.float32)
    sig_gate = jax.nn.sigmoid(gate_pre)
    active = gate_pre * sig_gate * upward
    scaled = (p_rows.astype(jnp.float32)[:, None] * dy_rows.astype(jnp.float32)).astype(jnp.bfloat16)
    contract_rows = (((0,), (0,)), ((), ()))
    grad_down = lax.dot_general(active.astype(jnp.bfloat16), scaled, contract_rows, preferred_element_type=jnp.float32)
    back_act = lax.dot_general(dy_rows, w_d, contract_d, preferred_element_type=jnp.float32)
    d_prob = jnp.sum(active * back_act, axis=1)
    return gate_pre, upward, sig_gate, back_act, grad_down, d_prob


def inner_part(x_rows, p_rows, gate_pre, upward, sig_gate, back_act, w_g, w_u):
    scaled_back = p_rows.astype(jnp.float32)[:, None] * back_act
    d_gate = (scaled_back * upward * (sig_gate + gate_pre * sig_gate * (1.0 - sig_gate))).astype(jnp.bfloat16)
    d_up = (scaled_back * gate_pre * sig_gate).astype(jnp.bfloat16)
    contract_rows = (((0,), (0,)), ((), ()))
    grad_gate = lax.dot_general(d_gate, x_rows, contract_rows, preferred_element_type=jnp.float32)
    grad_up = lax.dot_general(d_up, x_rows, contract_rows, preferred_element_type=jnp.float32)
    d_input = jnp.dot(d_gate, w_g, preferred_element_type=jnp.float32) + jnp.dot(d_up, w_u, preferred_element_type=jnp.float32)
    return grad_gate, grad_up, d_input


def reference(tokens, grad_out, routes, gate_probs, w_gate, w_up, w_down):
    n_blocks = N_EXPERT * N_DP
    per_block = 2 * TOK_DEV
    flat_route = routes.reshape(n_blocks, per_block)
    onehot = (flat_route[:, :, None] == jnp.arange(EXPERTS, dtype=jnp.int32)[None, None, :]).astype(jnp.int32)
    slot_rank = jnp.sum(jnp.cumsum(onehot, axis=1) * onehot, axis=2) - 1
    block_ids = jnp.arange(n_blocks, dtype=jnp.int32)[:, None]
    target = (flat_route * (n_blocks * CAP) + block_ids * CAP + slot_rank).reshape(-1).astype(jnp.int32)
    slot_table = jnp.full((EXPERTS * n_blocks * CAP,), 2 * TOKENS, jnp.int32)
    slot_table = slot_table.at[target].set(jnp.arange(2 * TOKENS, dtype=jnp.int32)).reshape(EXPERTS, n_blocks * CAP)
    model_width = tokens.shape[1]
    x_ext = jnp.concatenate([tokens, jnp.zeros((1, model_width), tokens.dtype)], axis=0)
    dy_ext = jnp.concatenate([grad_out, jnp.zeros((1, model_width), grad_out.dtype)], axis=0)
    p_ext = jnp.concatenate([gate_probs.reshape(-1), jnp.zeros((1,), gate_probs.dtype)], axis=0)

    def per_expert(totals, inputs):
        dx_acc, dp_acc = totals
        slots, w_g, w_u, w_d = inputs
        token_of = (slots // 2).astype(jnp.int32)
        x_rows = x_ext[token_of]
        dy_rows = dy_ext[token_of]
        p_rows = p_ext[slots]
        gate_pre, upward, sig_gate, back_act, grad_down, d_prob = forward_part(x_rows, dy_rows, p_rows, w_g, w_u, w_d)
        grad_gate, grad_up, d_input = inner_part(x_rows, p_rows, gate_pre, upward, sig_gate, back_act, w_g, w_u)
        dx_acc = dx_acc.at[token_of].add(d_input)
        dp_acc = dp_acc.at[slots].set(d_prob)
        return (dx_acc, dp_acc), (grad_gate, grad_up, grad_down)

    initial = (jnp.zeros((TOKENS + 1, model_width), jnp.float32), jnp.zeros((2 * TOKENS + 1,), jnp.float32))
    (dx_acc, dp_acc), grads = lax.scan(per_expert, initial, (slot_table, w_gate, w_up, w_down))
    d_tokens = dx_acc[:TOKENS].astype(jnp.bfloat16)
    d_probs = dp_acc[:2 * TOKENS].reshape(TOKENS, 2)
    return d_tokens, d_probs, grads[0], grads[1], grads[2]
```

```python
import jax
import jax.numpy as jnp
from jax import lax
from jax.sharding import PartitionSpec as P

F32 = jnp.float32
BF16 = jnp.bfloat16
CONTRACT_D = (((1,), (1,)), ((), ()))
CONTRACT_ROWS = (((0,), (0,)), ((), ()))


def per_device(tokens, grad_out, routes, gate_probs, w_gate, w_up, w_down):
    tok_count, model_width = tokens.shape
    n_expert = lax.axis_size("expert")
    capacity = 4 * tok_count // n_expert
    row_total = n_expert * capacity

    def swap(a):
        return lax.all_to_all(a, "expert", split_axis=0, concat_axis=0, tiled=True)

    experts = jnp.arange(n_expert, dtype=jnp.int32)
    hot = [(routes[:, k][None, :] == experts[:, None]) for k in range(2)]
    before = (
        jnp.arange(tok_count)[:, None] < jnp.arange(tok_count)[None, :]
    ).astype(BF16)
    ranks = [jnp.dot(h.astype(BF16), before, preferred_element_type=F32) for h in hot]
    ranks[1] = ranks[1] + jnp.sum(hot[0].astype(F32), axis=1, keepdims=True)
    base = (experts * capacity)[:, None]
    target = [
        jnp.sum(jnp.where(h, r.astype(jnp.int32) + base, 0), axis=0)
        for h, r in zip(hot, ranks)
    ]
    slots = jnp.arange(row_total, dtype=jnp.int32)
    pick = [slots[:, None] == t[None, :] for t in target]
    probs = gate_probs.astype(F32)
    take = jnp.where(pick[0] | pick[1], 1.0, 0.0).astype(BF16)
    take_scaled = (
        jnp.where(pick[0], probs[:, 0][None, :], 0.0)
        + jnp.where(pick[1], probs[:, 1][None, :], 0.0)
    ).astype(BF16)
    x_send = jnp.dot(take, tokens, preferred_element_type=F32).astype(BF16)
    s_send = jnp.dot(take_scaled, grad_out, preferred_element_type=F32).astype(BF16)
    x_rows = swap(x_send.reshape(n_expert, capacity, model_width)).reshape(
        row_total, model_width
    )
    s_rows = swap(s_send.reshape(n_expert, capacity, model_width)).reshape(
        row_total, model_width
    )
    w_g, w_u, w_d = w_gate[0], w_up[0], w_down[0]

    def dot(a, b, dims):
        return lax.dot_general(a, b, dims, preferred_element_type=F32)

    gate_pre = dot(x_rows, w_g, CONTRACT_D)
    upward = dot(x_rows, w_u, CONTRACT_D)
    scaled_back = dot(s_rows, w_d, CONTRACT_D)
    sig = jax.nn.sigmoid(gate_pre)
    silu = gate_pre * sig
    active = silu * upward
    dprob_rows = jnp.sum(active * scaled_back, axis=1)
    d_gate = (scaled_back * upward * (sig + silu * (1.0 - sig))).astype(BF16)
    d_up = (scaled_back * silu).astype(BF16)

    def reduce_rows(a):
        return lax.psum_scatter(
            a.astype(BF16), "dp", scatter_dimension=0, tiled=True
        ).astype(F32)[None]

    grad_d = reduce_rows(dot(active.astype(BF16), s_rows, CONTRACT_ROWS))
    grad_g = reduce_rows(dot(d_gate, x_rows, CONTRACT_ROWS))
    grad_u = reduce_rows(dot(d_up, x_rows, CONTRACT_ROWS))
    d_rows = (
        jnp.dot(d_gate, w_g, preferred_element_type=F32)
        + jnp.dot(d_up, w_u, preferred_element_type=F32)
    ).astype(BF16)
    dx_back = swap(d_rows.reshape(n_expert, capacity, model_width)).reshape(
        row_total, model_width
    )
    dp_back = swap(dprob_rows.reshape(n_expert, capacity)).reshape(row_total)
    d_tokens = dot(take, dx_back, CONTRACT_ROWS).astype(BF16)
    d_probs = (
        jnp.stack(
            [jnp.sum(jnp.where(m, dp_back[:, None], 0.0), axis=0) for m in pick], axis=1
        )
        / probs
    )
    return (d_tokens, d_probs, grad_g, grad_u, grad_d)


def solution(mesh):
    rows, experts = P(("expert", "dp"), None), P("expert", None, None)
    split = P("expert", "dp", None)
    return jax.shard_map(
        per_device,
        mesh=mesh,
        in_specs=(rows, rows, rows, rows, experts, experts, experts),
        out_specs=(rows, rows, split, split, split),
        check_vma=False,
    )
```

```python
import functools

import jax
import jax.numpy as jnp
from jax import lax
from jax.experimental import pallas as pl
from jax.experimental.pallas import tpu as pltpu
from jax.sharding import PartitionSpec as P

F32 = jnp.float32
BF16 = jnp.bfloat16
MESH = pl.DeviceIdType.MESH
NT = (((1,), (1,)), ((), ()))
TN = (((0,), (0,)), ((), ()))
NN = (((1,), (0,)), ((), ()))

RINGS = (
    ((2, 0), (0, 2), (2, 2)),
    ((2, 1), (1, 2), (2, 3), (3, 2)),
    ((1, 1), (3, 3), (1, 3), (3, 1)),
    ((1, 0), (0, 1), (3, 0), (0, 3)),
)
SHIFTS = [(0, 0, 0), (0, 0, 1)] + [
    (dx, dy, dc) for ring in RINGS for dc in (0, 1) for dx, dy in ring
]
CAP = 32
GROUP = 8
ROWS = GROUP * CAP
HALVES = 8
PIECES = 4


def dot(a, b, dims):
    return lax.dot_general(a, b, dims, preferred_element_type=F32)


def kernel(
    tok_ref,
    dy_ref,
    routes_ref,
    probs_ref,
    wg_hbm,
    wu_hbm,
    wd_hbm,
    dtok_ref,
    dprob_ref,
    gg_ref,
    gu_ref,
    gd_ref,
    pick,
    pick_scaled,
    xs,
    ss,
    xr,
    sr,
    wgu,
    wd,
    dgu,
    act,
    back_s,
    back_r,
    far_r,
    near_r,
    w_sem,
    fwd_s,
    fwd_r,
    back_ss,
    back_rs,
    sum_s,
    sum_r,
):
    me, z = lax.axis_index("expert"), lax.axis_index("dp")
    cx, cy, core = me // 8, (me // 2) % 4, me % 2
    up, down, across = (z + 1) % 4, (z + 3) % 4, (z + 2) % 4
    n_shift = len(SHIFTS)
    groups = n_shift // GROUP
    width = tok_ref.shape[1]
    half = wd.shape[1]

    def owner(i):
        dx, dy, dc = SHIFTS[i]
        return ((cx + dx) % 4) * 8 + ((cy + dy) % 4) * 2 + (core + dc) % 2

    def source(i):
        dx, dy, dc = SHIFTS[i]
        return ((cx + 4 - dx) % 4) * 8 + ((cy + 4 - dy) % 4) * 2 + (core + dc) % 2

    barrier = pltpu.get_barrier_semaphore()
    for i in range(1, n_shift):
        pl.semaphore_signal(barrier, inc=1, device_id=(owner(i), z), device_id_type=MESH)
    for other in (up, down):
        pl.semaphore_signal(barrier, inc=1, device_id=(me, other), device_id_type=MESH)

    loads = [
        pltpu.make_async_copy(wg_hbm, wgu.at[:, 0:half], w_sem.at[0]),
        pltpu.make_async_copy(wu_hbm, wgu.at[:, half : 2 * half], w_sem.at[1]),
        pltpu.make_async_copy(wd_hbm, wd, w_sem.at[2]),
    ]
    for load in loads:
        load.start()

    n_tok = tok_ref.shape[0]
    lane = lax.broadcasted_iota(jnp.int32, (n_tok, 128), 1)
    place = jnp.zeros((1, 128), jnp.int32)
    for i in range(1, n_shift):
        place = place + jnp.where(lane[0:1] == owner(i), i * CAP, 0)
    earlier = (
        lax.broadcasted_iota(jnp.int32, (n_tok, n_tok), 0)
        > lax.broadcasted_iota(jnp.int32, (n_tok, n_tok), 1)
    )
    earlier = jnp.where(earlier, 1.0, 0.0).astype(BF16)
    slot = lax.broadcasted_iota(jnp.int32, (n_tok, n_shift * CAP), 1)
    offset = place.astype(F32)
    scaled = jnp.zeros((n_tok, n_shift * CAP), F32)
    for k in range(2):
        named = lane == routes_ref[:, k : k + 1]
        hot = jnp.where(named, 1.0, 0.0)
        rank = dot(earlier, hot.astype(BF16), NN) + offset
        offset = offset + jnp.sum(hot, axis=0, keepdims=True)
        target = jnp.sum(jnp.where(named, rank, 0.0), axis=1, keepdims=True)
        chosen = slot == target.astype(jnp.int32)
        pick[k] = jnp.where(chosen, 1.0, 0.0).astype(BF16)
        scaled = scaled + jnp.where(chosen, probs_ref[:, k : k + 1].astype(F32), 0.0)
    pick_scaled[...] = scaled.astype(BF16)

    def forward_copy(i, piece, device):
        src, dst = (xs, xr) if piece < PIECES // 2 else (ss, sr)
        step = 2 * CAP // PIECES
        at = pl.ds(i * CAP + (piece % (PIECES // 2)) * step, step)
        return pltpu.make_async_remote_copy(
            src_ref=src.at[at],
            dst_ref=dst.at[at],
            send_sem=fwd_s.at[i, piece],
            recv_sem=fwd_r.at[i, piece],
            device_id=(device, z),
            device_id_type=MESH,
        )

    for g in range(groups):
        at = slice(g * ROWS, (g + 1) * ROWS)
        both = pick[0, :, at] + pick[1, :, at]
        xs[at] = dot(both, tok_ref[...], TN).astype(BF16)
        ss[at] = dot(pick_scaled[:, at], dy_ref[...], TN).astype(BF16)
        if g == 0:
            pl.semaphore_wait(barrier, n_shift + 1)
        for piece in range(PIECES):
            for i in range(max(1, g * GROUP), (g + 1) * GROUP):
                forward_copy(i, piece, owner(i)).start()
    xr[0:CAP] = xs[0:CAP]
    sr[0:CAP] = ss[0:CAP]
    for load in loads:
        load.wait()

    def back_copy(i, device):
        at = slice(i * CAP, (i + 1) * CAP)
        return pltpu.make_async_remote_copy(
            src_ref=back_s.at[at],
            dst_ref=back_r.at[at],
            send_sem=back_ss.at[i],
            recv_sem=back_rs.at[i],
            device_id=(device, z),
            device_id_type=MESH,
        )

    def row_gradients(g):
        at = pl.ds(pl.multiple_of(g * ROWS, ROWS), ROWS)
        lhs = dgu[:, :, at].reshape(HALVES * 2 * half, ROWS)

        def tile(n, _):
            cols = pl.ds(pl.multiple_of(n * 512, 512), 512)
            rhs = wgu[:, :, cols].reshape(HALVES * 2 * half, 512)
            back_s[at, cols] = dot(lhs, rhs, TN).astype(BF16)
            return 0

        lax.fori_loop(0, width // 512, tile, 0)

    def work(g, _):
        def arrived(i, _):
            for piece in range(PIECES):
                forward_copy(i, piece, me).wait_recv()
            return 0

        lax.fori_loop(jnp.maximum(g * GROUP, 1), (g + 1) * GROUP, arrived, 0)
        at = pl.ds(pl.multiple_of(g * ROWS, ROWS), ROWS)

        def tile(h, total):
            pre = dot(wgu[h], xr[at], NT)
            scaled_back = dot(wd[h], sr[at], NT)
            gate, upward = pre[0:half], pre[half : 2 * half]
            sig = jax.nn.sigmoid(gate)
            silu = gate * sig
            active = silu * upward
            act[h, :, at] = active.astype(BF16)
            d_gate = scaled_back * upward * (sig + silu * (1.0 - sig))
            dgu[h, 0:half, at] = d_gate.astype(BF16)
            dgu[h, half : 2 * half, at] = (scaled_back * silu).astype(BF16)
            return total + jnp.sum(active * scaled_back, axis=0, keepdims=True)

        total = lax.fori_loop(0, HALVES, tile, jnp.zeros((1, ROWS), F32))
        high = total.astype(BF16).astype(F32)
        line = lax.broadcasted_iota(jnp.int32, (128, ROWS), 0)
        pair = jnp.where(line == 0, high, jnp.where(line == 1, total - high, 0.0))
        back_s[at, width : width + 128] = pair.T.astype(BF16)

        @pl.when(g < groups - 1)
        def _():
            row_gradients(g)

        return 0

    lax.fori_loop(0, groups, work, 0)

    last = (groups - 1) * GROUP
    for i in range(1, last):
        back_copy(i, source(i)).start()

    def sent(i, _):
        for piece in range(PIECES):
            forward_copy(i, piece, me).wait_send()
        return 0

    lax.fori_loop(1, n_shift, sent, 0)

    def half_shard(h, finish):
        def tile(n, _):
            cols = pl.ds(pl.multiple_of(n * 512, 512), 512)
            finish(0, cols, dot(dgu[h], xr[:, cols], NN))
            finish(2 * half, cols, dot(act[h], sr[:, cols], NN))
            return 0

        lax.fori_loop(0, width // 512, tile, 0)

    block = 3 * half

    def sum_copy(i, src, dst, device):
        return pltpu.make_async_remote_copy(
            src_ref=src,
            dst_ref=dst,
            send_sem=sum_s.at[i],
            recv_sem=sum_r.at[i],
            device_id=(me, device),
            device_id_type=MESH,
        )

    def send_half(i, h, src, first, dst, device, add=None):
        def finish(row, cols, value):
            if add is not None:
                value = value + add[pl.ds(row, value.shape[0]), cols].astype(F32)
            src[pl.ds(first + row, value.shape[0]), cols] = value.astype(BF16)

        half_shard(h, finish)
        copy = sum_copy(i, src.at[pl.ds(first, block)], dst, device)
        copy.start()
        return copy

    far_up = send_half(0, 2 * across, xs, 0, far_r.at[0], up)
    far_down = send_half(1, 2 * across + 1, xs, block, far_r.at[1], down)
    near = [
        send_half(2, 2 * up + 1, xs, 2 * block, near_r.at[0, 1], up),
        send_half(3, 2 * down, ss, 0, near_r.at[1, 0], down),
    ]
    row_gradients(groups - 1)
    for i in range(last, n_shift):
        back_copy(i, source(i)).start()
    far_up.wait_recv()
    near.append(send_half(4, 2 * up, ss, block, near_r.at[0, 0], up, far_r.at[0]))
    far_down.wait_recv()
    near.append(
        send_half(5, 2 * down + 1, ss, 2 * block, near_r.at[1, 1], down, far_r.at[1])
    )

    for part in range(2):

        def keep(row, cols, value, part=part):
            low = slice(part * half, (part + 1) * half)
            if row == 0:
                gg_ref[low, cols] = value[0:half]
                gu_ref[low, cols] = value[half : 2 * half]
            else:
                gd_ref[low, cols] = value

        half_shard(2 * z + part, keep)

    back_r[0:CAP] = back_s[0:CAP]
    for i in range(1, n_shift):
        back_copy(i, me).wait_recv()

    def combine(n, _):
        cols = pl.ds(pl.multiple_of(n * 512, 512), 512)
        both = pick[0] + pick[1]
        dtok_ref[:, cols] = dot(both, back_r[:, cols], NN).astype(BF16)
        return 0

    lax.fori_loop(0, width // 512, combine, 0)
    for k in range(2):
        terms = dot(pick[k], back_r[:, width : width + 128], NN)
        dprob_ref[:, k : k + 1] = jnp.sum(terms, axis=1, keepdims=True) / probs_ref[
            :, k : k + 1
        ].astype(F32)

    for copy, part in ((near[0], 1), (near[1], 0), (near[2], 0), (near[3], 1)):
        copy.wait_recv()
    for part in range(2):
        low = slice(part * half, (part + 1) * half)
        for j, out in enumerate((gg_ref, gu_ref, gd_ref)):
            rows = slice(j * half, (j + 1) * half)
            out[low] = (
                out[low]
                + near_r[0, part, rows].astype(F32)
                + near_r[1, part, rows].astype(F32)
            )
    for copy in [far_up, far_down] + near:
        copy.wait_send()
    for i in range(1, n_shift):
        back_copy(i, me).wait_send()


def per_device(tokens, grad_out, routes, gate_probs, w_gate, w_up, w_down):
    n_tok, width = tokens.shape
    hidden = w_gate.shape[1]
    half = hidden // HALVES
    slots = len(SHIFTS) * CAP
    vmem = pl.BlockSpec(memory_space=pltpu.VMEM)
    hbm = pl.BlockSpec(memory_space=pl.ANY)
    weights = [w.reshape(HALVES, half, width) for w in (w_gate, w_up, w_down)]
    shard = jax.ShapeDtypeStruct((hidden // 4, width), F32)
    dma = pltpu.SemaphoreType.DMA
    d_tokens, d_probs, grad_g, grad_u, grad_d = pl.pallas_call(
        kernel,
        out_shape=(
            jax.ShapeDtypeStruct((n_tok, width), BF16),
            jax.ShapeDtypeStruct((n_tok, 2), F32),
            shard,
            shard,
            shard,
        ),
        in_specs=[vmem] * 4 + [hbm] * 3,
        out_specs=[vmem] * 5,
        scratch_shapes=[
            pltpu.VMEM((2, n_tok, slots), BF16),
            pltpu.VMEM((n_tok, slots), BF16),
            pltpu.VMEM((slots, width), BF16),
            pltpu.VMEM((slots, width), BF16),
            pltpu.VMEM((slots, width), BF16),
            pltpu.VMEM((slots, width), BF16),
            pltpu.VMEM((HALVES, 2 * half, width), BF16),
            pltpu.VMEM((HALVES, half, width), BF16),
            pltpu.VMEM((HALVES, 2 * half, slots), BF16),
            pltpu.VMEM((HALVES, half, slots), BF16),
            pltpu.VMEM((slots, width + 128), BF16),
            pltpu.VMEM((slots, width + 128), BF16),
            pltpu.VMEM((2, 3 * half, width), BF16),
            pltpu.VMEM((2, 2, 3 * half, width), BF16),
            dma((3,)),
            dma((len(SHIFTS), PIECES)),
            dma((len(SHIFTS), PIECES)),
            dma((len(SHIFTS),)),
            dma((len(SHIFTS),)),
            dma((6,)),
            dma((6,)),
        ],
        compiler_params=pltpu.CompilerParams(
            collective_id=0, has_side_effects=True, vmem_limit_bytes=62 << 20
        ),
        name="routed_backward",
    )(tokens, grad_out, routes, gate_probs, *weights)
    return d_tokens, d_probs, grad_g[None], grad_u[None], grad_d[None]


def solution(mesh):
    rows, experts = P(("expert", "dp"), None), P("expert", None, None)
    split = P("expert", "dp", None)
    return jax.shard_map(
        per_device,
        mesh=mesh,
        in_specs=(rows, rows, rows, rows, experts, experts, experts),
        out_specs=(rows, rows, split, split, split),
        check_vma=False,
    )
```

```python
import functools

import jax
import jax.numpy as jnp
from jax import lax
from jax.experimental import pallas as pl
from jax.experimental.pallas import tpu as pltpu
from jax.sharding import PartitionSpec as P

F32 = jnp.float32
BF16 = jnp.bfloat16
MESH = pl.DeviceIdType.MESH
NT = (((1,), (1,)), ((), ()))
TN = (((0,), (0,)), ((), ()))
NN = (((1,), (0,)), ((), ()))

RINGS = (
    ((2, 0), (0, 2), (2, 2)),
    ((2, 1), (1, 2), (2, 3), (3, 2)),
    ((1, 1), (3, 3), (1, 3), (3, 1)),
    ((1, 0), (0, 1), (3, 0), (0, 3)),
)
SHIFTS = [(0, 0, 0), (0, 0, 1)] + [
    (dx, dy, dc) for ring in RINGS for dc in (0, 1) for dx, dy in ring
]
CAP = 32
GROUP = 8
ROWS = GROUP * CAP
COLS = 512
HALVES = 8


def dot(a, b, dims):
    return lax.dot_general(a, b, dims, preferred_element_type=F32)


def kernel(
    tok_ref,
    dy_ref,
    routes_ref,
    probs_ref,
    wg_hbm,
    wu_hbm,
    wd_hbm,
    dtok_ref,
    dprob_ref,
    own_gu_hbm,
    own_d_hbm,
    near_gu,
    near_d,
    pick,
    pick_scaled,
    xs,
    ss,
    xr,
    sr,
    wgu,
    wd,
    dgu,
    act,
    slope,
    silus,
    backs,
    own_d,
    back_s,
    back_r,
    far_gu,
    far_d,
    w_sem,
    x_s,
    x_r,
    s_s,
    s_r,
    back_ss,
    back_rs,
    gu_s,
    gu_r,
    d_s,
    d_r,
    own_sem,
):
    me, z = lax.axis_index("expert"), lax.axis_index("dp")
    cx, cy, core = me // 8, (me // 2) % 4, me % 2
    up, down, across = (z + 1) % 4, (z + 3) % 4, (z + 2) % 4
    n_shift = len(SHIFTS)
    groups = n_shift // GROUP
    n_tok, width = tok_ref.shape
    chunks = width // COLS
    half = wd.shape[0] // HALVES

    def owner(i):
        dx, dy, dc = SHIFTS[i]
        return ((cx + dx) % 4) * 8 + ((cy + dy) % 4) * 2 + (core + dc) % 2

    def source(i):
        dx, dy, dc = SHIFTS[i]
        return ((cx + 4 - dx) % 4) * 8 + ((cy + 4 - dy) % 4) * 2 + (core + dc) % 2

    def remote(src, dst, send_sem, recv_sem, device):
        return pltpu.make_async_remote_copy(
            src_ref=src,
            dst_ref=dst,
            send_sem=send_sem,
            recv_sem=recv_sem,
            device_id=device,
            device_id_type=MESH,
        )

    barrier = pltpu.get_barrier_semaphore()
    for i in range(1, n_shift):
        pl.semaphore_signal(barrier, inc=1, device_id=(owner(i), z), device_id_type=MESH)
    for other in (up, down):
        pl.semaphore_signal(barrier, inc=1, device_id=(me, other), device_id_type=MESH)

    loads = [
        pltpu.make_async_copy(wd_hbm, wd, w_sem.at[0]),
    ]
    for h in range(HALVES):
        for j, w in enumerate((wg_hbm, wu_hbm)):
            loads.append(
                pltpu.make_async_copy(
                    w.at[h * half : (h + 1) * half],
                    wgu.at[(2 * h + j) * half : (2 * h + j + 1) * half],
                    w_sem.at[1 + 2 * h + j],
                )
            )
    for load in loads:
        load.start()

    line = lax.broadcasted_iota(jnp.int32, (128, n_tok), 0)
    routes = routes_ref[...].astype(F32)
    probs = probs_ref[...].astype(F32)
    table = jnp.where(line == 0, routes[0:1], routes[1:2])
    table = jnp.where(line == 2, probs[0:1], table)
    table = jnp.where(line == 3, probs[1:2], table).T
    lane = lax.broadcasted_iota(jnp.int32, (n_tok, 128), 1)
    place = jnp.zeros((1, 128), jnp.int32)
    for i in range(1, n_shift):
        place = place + jnp.where(lane[0:1] == owner(i), i * CAP, 0)
    earlier = (
        lax.broadcasted_iota(jnp.int32, (n_tok, n_tok), 0)
        > lax.broadcasted_iota(jnp.int32, (n_tok, n_tok), 1)
    )
    earlier = jnp.where(earlier, 1.0, 0.0).astype(BF16)
    slot = lax.broadcasted_iota(jnp.int32, (n_tok, n_shift * CAP), 1)
    offset = place.astype(F32)
    scaled = jnp.zeros((n_tok, n_shift * CAP), F32)
    for k in range(2):
        named = lane == table[:, k : k + 1].astype(jnp.int32)
        hot = jnp.where(named, 1.0, 0.0)
        rank = dot(earlier, hot.astype(BF16), NN) + offset
        offset = offset + jnp.sum(hot, axis=0, keepdims=True)
        target = jnp.sum(jnp.where(named, rank, 0.0), axis=1, keepdims=True)
        chosen = slot == target.astype(jnp.int32)
        pick[k] = jnp.where(chosen, 1.0, 0.0).astype(BF16)
        scaled = scaled + jnp.where(chosen, table[:, 2 + k : 3 + k], 0.0)
    pick_scaled[...] = scaled.astype(BF16)

    for g in range(groups):
        at = slice(g * ROWS, (g + 1) * ROWS)
        both = pick[0, :, at] + pick[1, :, at]
        for c in range(chunks):
            cols = slice(c * COLS, (c + 1) * COLS)
            xs[c, at] = dot(both, tok_ref[:, cols], TN).astype(BF16)
        if g == 0:
            pl.semaphore_wait(barrier, n_shift + 1)
        for c in range(chunks):
            for i in range(max(1, g * GROUP), (g + 1) * GROUP):
                rows = slice(i * CAP, (i + 1) * CAP)
                remote(
                    xs.at[c, rows], xr.at[c, rows], x_s, x_r.at[g], (owner(i), z)
                ).start()
    for c in range(chunks):
        cols = slice(c * COLS, (c + 1) * COLS)
        for g in range(groups):
            at = slice(g * ROWS, (g + 1) * ROWS)
            ss[c, at] = dot(pick_scaled[:, at], dy_ref[:, cols], TN).astype(BF16)
        for i in range(1, n_shift):
            rows = slice(i * CAP, (i + 1) * CAP)
            remote(
                ss.at[c, rows], sr.at[c, rows], s_s, s_r.at[c], (owner(i), z)
            ).start()
    for c in range(chunks):
        xr[c, 0:CAP] = xs[c, 0:CAP]
        sr[c, 0:CAP] = ss[c, 0:CAP]
    for load in loads:
        load.wait()

    for g in range(groups):
        first = CAP if g == 0 else g * ROWS
        took = slice(first, (g + 1) * ROWS)
        remote(xs.at[:, took], xr.at[:, took], x_s, x_r.at[g], (me, z)).wait_recv()
        at = slice(g * ROWS, (g + 1) * ROWS)

        def project(t, _, at=at):
            rows = pl.ds(pl.multiple_of(t * 4 * half, 4 * half), 4 * half)
            pre = jnp.zeros((4 * half, ROWS), F32)
            for c in range(chunks):
                cols = slice(c * COLS, (c + 1) * COLS)
                pre = pre + dot(wgu[rows, cols], xr[c, at], NT)
            for j in range(2):
                gate = pre[2 * j * half : (2 * j + 1) * half]
                upward = pre[(2 * j + 1) * half : (2 * j + 2) * half]
                into = pl.ds(pl.multiple_of((2 * t + j) * half, half), half)
                sig = jax.nn.sigmoid(gate)
                silu = gate * sig
                act[into, at] = (silu * upward).astype(BF16)
                slope[into, at] = upward * (sig + silu * (1.0 - sig))
                silus[into, at] = silu
            return 0

        lax.fori_loop(0, HALVES // 2, project, 0)

    sent = slice(CAP, n_shift * CAP)
    remote(xs.at[:, sent], xr.at[:, sent], x_s, x_r.at[0], (me, z)).wait_send()

    def part_rows(h, size):
        return pl.ds(pl.multiple_of(h * size, size), size)

    def down_half(h, c):
        return dot(act[part_rows(h, half)], sr[c], NN)

    D_ROWS = [slice(k * half, (k + 1) * half) for k in range(6)]

    def down_copy(k, c):
        dst = (
            far_d.at[0, c],
            far_d.at[1, c],
            near_d.at[0, 1, c],
            near_d.at[1, 0, c],
            near_d.at[0, 0, c],
            near_d.at[1, 1, c],
        )[k]
        return remote(
            xs.at[c, D_ROWS[k]],
            dst,
            d_s.at[k, c],
            d_r.at[k, c],
            (me, up if k % 2 == 0 else down),
        )

    halves = (2 * across, 2 * across + 1, 2 * up + 1, 2 * down, 2 * up, 2 * down + 1)

    def down_first(c):
        for k in range(4):
            xs[c, D_ROWS[k]] = down_half(halves[k], c).astype(BF16)
            down_copy(k, c).start()
        for part in range(2):
            own_d[(part * chunks + c) * half : (part * chunks + c + 1) * half] = (
                down_half(2 * z + part, c)
            )

    def down_second(c):
        for k in range(4, 6):
            value = down_half(halves[k], c)
            down_copy(k - 4, c).wait_recv()
            xs[c, D_ROWS[k]] = (value + far_d[k - 4, c].astype(F32)).astype(BF16)
            down_copy(k, c).start()

    def chunk_arrived(c):
        remote(ss.at[c, sent], sr.at[c, sent], s_s, s_r.at[c], (me, z)).wait_recv()

    big = 4 * half
    for c in range(chunks - 1):
        cols = slice(c * COLS, (c + 1) * COLS)
        chunk_arrived(c)
        down_first(c)

        def project_back(t, _, c=c, cols=cols):
            rows = part_rows(t, big)
            value = dot(wd[rows, cols], sr[c], NT)
            backs[rows] = value if c == 0 else backs[rows] + value
            return 0

        lax.fori_loop(0, HALVES // 4, project_back, 0)
        down_second(c)

    chunk_arrived(chunks - 1)
    remote(ss.at[:, sent], sr.at[:, sent], s_s, s_r.at[0], (me, z)).wait_send()
    last_cols = slice((chunks - 1) * COLS, chunks * COLS)

    def finish_half(h):
        rows = part_rows(h, half)
        back = backs[rows] + dot(wd[rows, last_cols], sr[chunks - 1], NT)
        dgu[pl.ds(pl.multiple_of(2 * h * half, 2 * half), half)] = (
            back * slope[rows]
        ).astype(BF16)
        dgu[pl.ds(pl.multiple_of((2 * h + 1) * half, half), half)] = (
            back * silus[rows]
        ).astype(BF16)
        return jnp.sum(act[rows].astype(F32) * back, axis=0, keepdims=True)

    def gate_up_half(h, c):
        return dot(dgu[part_rows(h, 2 * half)], xr[c], NN)

    def gate_up_copy(k, c):
        dst = (
            far_gu.at[0, c],
            far_gu.at[1, c],
            near_gu.at[0, 1, c],
            near_gu.at[1, 0, c],
            near_gu.at[0, 0, c],
            near_gu.at[1, 1, c],
        )[k]
        size = 2 * half
        if k < 5:
            src = ss.at[c, k * size : (k + 1) * size]
        else:
            src = xs.at[c, 6 * half : 6 * half + size]
        return src, remote(
            src,
            dst,
            gu_s.at[k, c],
            gu_r.at[k, c],
            (me, up if k % 2 == 0 else down),
        )

    def send_gate_up(k):
        def tile(c, _):
            value = gate_up_half(halves[k], c)
            src, copy = gate_up_copy(k, c)
            if k >= 4:
                gate_up_copy(k - 4, c)[1].wait_recv()
                value = value + far_gu[k - 4, c].astype(F32)
            src[...] = value.astype(BF16)
            copy.start()
            return 0

        lax.fori_loop(0, chunks, tile, 0)

    total = finish_half(halves[0])
    send_gate_up(0)
    total = total + finish_half(halves[1])
    send_gate_up(1)
    total = lax.fori_loop(
        2, HALVES, lambda i, t: t + finish_half((2 * across + i) % HALVES), total
    )
    high = total.astype(BF16).astype(F32)
    for g in range(groups):
        at = slice(g * ROWS, (g + 1) * ROWS)
        line = lax.broadcasted_iota(jnp.int32, (128, ROWS), 0)
        pair = jnp.where(line == 0, high[:, at], 0.0)
        pair = jnp.where(line == 1, (total - high)[:, at], pair)
        back_s[at, width : width + 128] = pair.T.astype(BF16)

    def back_copy(i, piece, device):
        at = slice(i * CAP + piece * CAP // 2, i * CAP + (piece + 1) * CAP // 2)
        return remote(back_s.at[at], back_r.at[at], back_ss, back_rs, (device, z))

    def return_rows(g):
        at = slice(g * ROWS, (g + 1) * ROWS)

        def tile(n, _):
            cols = pl.ds(pl.multiple_of(n * COLS, COLS), COLS)
            back_s[at, cols] = dot(dgu[:, at], wgu[:, cols], TN).astype(BF16)
            return 0

        lax.fori_loop(0, chunks, tile, 0)
        for piece in range(2):
            for i in range(max(1, g * GROUP), (g + 1) * GROUP):
                back_copy(i, piece, source(i)).start()

    return_rows(0)
    send_gate_up(2)
    send_gate_up(3)
    for g in range(1, groups):
        return_rows(g)
    down_first(chunks - 1)
    send_gate_up(4)
    send_gate_up(5)
    down_second(chunks - 1)
    for part in range(2):

        def keep(c, _, part=part):
            value = gate_up_half(2 * z + part, c)
            rows = part_rows(part * chunks + c, half)
            slope[rows, 0:COLS] = value[0:half]
            slope[rows, COLS : 2 * COLS] = value[half : 2 * half]
            return 0

        lax.fori_loop(0, chunks, keep, 0)
    own = [
        pltpu.make_async_copy(slope, own_gu_hbm, own_sem.at[0]),
        pltpu.make_async_copy(own_d, own_d_hbm, own_sem.at[1]),
    ]
    for copy in own:
        copy.start()

    back_r[0:CAP] = back_s[0:CAP]
    remote(back_s.at[sent], back_r.at[sent], back_ss, back_rs, (me, z)).wait_recv()

    def combine(n, _):
        cols = pl.ds(pl.multiple_of(n * COLS, COLS), COLS)
        both = pick[0] + pick[1]
        dtok_ref[:, cols] = dot(both, back_r[:, cols], NN).astype(BF16)
        return 0

    lax.fori_loop(0, chunks, combine, 0)
    for k in range(2):
        terms = dot(pick[k], back_r[:, width : width + 128], NN).T
        dprob_ref[k : k + 1] = (
            jnp.sum(terms, axis=0, keepdims=True) / probs_ref[...].astype(F32)[k : k + 1]
        )

    def finish(c, _):
        for k in range(6):
            if k >= 2:
                down_copy(k, c).wait_recv()
                gate_up_copy(k, c)[1].wait_recv()
            down_copy(k, c).wait_send()
            gate_up_copy(k, c)[1].wait_send()
        return 0

    lax.fori_loop(0, chunks, finish, 0)
    for copy in own:
        copy.wait()
    remote(back_s.at[sent], back_r.at[sent], back_ss, back_rs, (me, z)).wait_send()


def add_up(own_gu, own_d, near_gu, near_d, tok_in, prob_in, tok, prob, gg, gu, gd):
    half = gg.shape[0]
    total = near_gu[0, 0, 0].astype(F32) + near_gu[1, 0, 0].astype(F32)
    gg[...] = own_gu[:, 0:COLS] + total[0:half]
    gu[...] = own_gu[:, COLS : 2 * COLS] + total[half : 2 * half]
    gd[...] = (
        own_d[...] + near_d[0, 0, 0].astype(F32) + near_d[1, 0, 0].astype(F32)
    )
    tok[...] = tok_in[...]
    prob[...] = prob_in[...]


def per_device(tokens, grad_out, routes, gate_probs, w_gate, w_up, w_down):
    n_tok, width = tokens.shape
    hidden = w_gate.shape[1]
    half = hidden // HALVES
    slots = len(SHIFTS) * CAP
    chunks = width // COLS
    vmem = pl.BlockSpec(memory_space=pltpu.VMEM)
    hbm = pl.BlockSpec(memory_space=pl.ANY)
    weights = [w[0] for w in (w_gate, w_up, w_down)]
    dma = pltpu.SemaphoreType.DMA
    d_tokens, d_probs, own_gu, own_d, near_gu, near_d = pl.pallas_call(
        kernel,
        out_shape=(
            jax.ShapeDtypeStruct((n_tok, width), BF16),
            jax.ShapeDtypeStruct((2, n_tok), F32),
            jax.ShapeDtypeStruct((hidden, 2 * COLS), F32),
            jax.ShapeDtypeStruct((hidden, COLS), F32),
            jax.ShapeDtypeStruct((2, 2, chunks, 2 * half, COLS), BF16),
            jax.ShapeDtypeStruct((2, 2, chunks, half, COLS), BF16),
        ),
        in_specs=[vmem] * 4 + [hbm] * 3,
        out_specs=[vmem] * 2 + [hbm] * 4,
        scratch_shapes=[
            pltpu.VMEM((2, n_tok, slots), BF16),
            pltpu.VMEM((n_tok, slots), BF16),
            pltpu.VMEM((chunks, slots, COLS), BF16),
            pltpu.VMEM((chunks, slots, COLS), BF16),
            pltpu.VMEM((chunks, slots, COLS), BF16),
            pltpu.VMEM((chunks, slots, COLS), BF16),
            pltpu.VMEM((2 * hidden, width), BF16),
            pltpu.VMEM((hidden, width), BF16),
            pltpu.VMEM((2 * hidden, slots), BF16),
            pltpu.VMEM((hidden, slots), BF16),
            pltpu.VMEM((hidden, slots), F32),
            pltpu.VMEM((hidden, slots), F32),
            pltpu.VMEM((hidden, slots), F32),
            pltpu.VMEM((hidden, COLS), F32),
            pltpu.VMEM((slots, width + 128), BF16),
            pltpu.VMEM((slots, width + 128), BF16),
            pltpu.VMEM((2, chunks, 2 * half, COLS), BF16),
            pltpu.VMEM((2, chunks, half, COLS), BF16),
            dma((1 + 2 * HALVES,)),
            dma,
            dma((len(SHIFTS) // GROUP,)),
            dma,
            dma((chunks,)),
            dma,
            dma,
            dma((6, chunks)),
            dma((6, chunks)),
            dma((6, chunks)),
            dma((6, chunks)),
            dma((2,)),
        ],
        compiler_params=pltpu.CompilerParams(
            collective_id=0, has_side_effects=True, vmem_limit_bytes=63 << 20
        ),
        name="routed_backward",
    )(tokens, grad_out, routes.T, gate_probs.T, *weights)
    step = lambda p, c: (p * chunks + c, 0)
    fixed = lambda p, c: (0, 0)
    tile = pl.BlockSpec((half, COLS), lambda p, c: (p, c))
    rows = pl.BlockSpec((n_tok // HALVES, width), step)
    row_probs = pl.BlockSpec((2, n_tok), fixed)
    shard = jax.ShapeDtypeStruct((hidden // 4, width), F32)
    d_tokens, d_probs, grad_g, grad_u, grad_d = pl.pallas_call(
        add_up,
        grid=(2, chunks),
        out_shape=(
            jax.ShapeDtypeStruct((n_tok, width), BF16),
            jax.ShapeDtypeStruct((2, n_tok), F32),
            shard,
            shard,
            shard,
        ),
        in_specs=[
            pl.BlockSpec((half, 2 * COLS), step),
            pl.BlockSpec((half, COLS), step),
            pl.BlockSpec((2, 1, 1, 2 * half, COLS), lambda p, c: (0, p, c, 0, 0)),
            pl.BlockSpec((2, 1, 1, half, COLS), lambda p, c: (0, p, c, 0, 0)),
            rows,
            row_probs,
        ],
        out_specs=[rows, row_probs, tile, tile, tile],
        name="add_up",
    )(own_gu, own_d, near_gu, near_d, d_tokens, d_probs)
    return d_tokens, d_probs.T, grad_g[None], grad_u[None], grad_d[None]


def solution(mesh):
    rows, experts = P(("expert", "dp"), None), P("expert", None, None)
    split = P("expert", "dp", None)
    return jax.shard_map(
        per_device,
        mesh=mesh,
        in_specs=(rows, rows, rows, rows, experts, experts, experts),
        out_specs=(rows, rows, split, split, split),
        check_vma=False,
    )
```

```python
import functools

import jax
import jax.numpy as jnp
from jax import lax
from jax.experimental import pallas as pl
from jax.experimental.pallas import tpu as pltpu
from jax.sharding import PartitionSpec as P

F32 = jnp.float32
BF16 = jnp.bfloat16
MESH = pl.DeviceIdType.MESH
NT = (((1,), (1,)), ((), ()))
TN = (((0,), (0,)), ((), ()))
NN = (((1,), (0,)), ((), ()))

RINGS = (
    ((2, 0), (0, 2), (2, 2)),
    ((2, 1), (1, 2), (2, 3), (3, 2)),
    ((1, 1), (3, 3), (1, 3), (3, 1)),
    ((1, 0), (0, 1), (3, 0), (0, 3)),
)
SHIFTS = [(0, 0, 0), (0, 0, 1)] + [
    (dx, dy, dc) for ring in RINGS for dc in (0, 1) for dx, dy in ring
]
CAP = 32
GROUP = 8
ROWS = GROUP * CAP
COLS = 512
PIECES = ((0, 0, 512), (1, 0, 512), (2, 0, 512), (3, 0, 256), (3, 256, 256))
HALVES = 8


def dot(a, b, dims):
    return lax.dot_general(a, b, dims, preferred_element_type=F32)


def kernel(
    tok_ref,
    dy_ref,
    routes_ref,
    probs_ref,
    wg_hbm,
    wu_hbm,
    wd_hbm,
    dtok_ref,
    dprob_ref,
    own_gu_hbm,
    own_d_hbm,
    near_gu,
    near_d,
    pick,
    pick_scaled,
    xs,
    ss,
    xr,
    sr,
    wgu,
    wd,
    dgu,
    act,
    slope,
    silus,
    backs,
    own_d,
    back_s,
    back_r,
    prob_s,
    prob_r,
    far_gu,
    far_d,
    mid_gu,
    mid_d,
    w_sem,
    x_s,
    x_r,
    s_s,
    s_r,
    back_ss,
    back_rs,
    prob_ss,
    prob_rs,
    gu_s,
    gu_r,
    d_s,
    d_r,
    own_sem,
):
    me, z = lax.axis_index("expert"), lax.axis_index("dp")
    cx, cy, core = me // 8, (me // 2) % 4, me % 2
    up, down, across = (z + 1) % 4, (z + 3) % 4, (z + 2) % 4
    n_shift = len(SHIFTS)
    groups = n_shift // GROUP
    n_tok, width = tok_ref.shape
    chunks = width // COLS
    half = wd.shape[0] // HALVES

    def owner(i):
        dx, dy, dc = SHIFTS[i]
        return ((cx + dx) % 4) * 8 + ((cy + dy) % 4) * 2 + (core + dc) % 2

    def source(i):
        dx, dy, dc = SHIFTS[i]
        return ((cx + 4 - dx) % 4) * 8 + ((cy + 4 - dy) % 4) * 2 + (core + dc) % 2

    def remote(src, dst, send_sem, recv_sem, device):
        return pltpu.make_async_remote_copy(
            src_ref=src,
            dst_ref=dst,
            send_sem=send_sem,
            recv_sem=recv_sem,
            device_id=device,
            device_id_type=MESH,
        )

    barrier = pltpu.get_barrier_semaphore()
    for i in range(1, n_shift):
        pl.semaphore_signal(barrier, inc=1, device_id=(owner(i), z), device_id_type=MESH)
    for other in (up, down):
        pl.semaphore_signal(barrier, inc=1, device_id=(me, other), device_id_type=MESH)

    loads = [
        pltpu.make_async_copy(wd_hbm, wd, w_sem.at[0]),
    ]
    for h in range(HALVES):
        for j, w in enumerate((wg_hbm, wu_hbm)):
            loads.append(
                pltpu.make_async_copy(
                    w.at[h * half : (h + 1) * half],
                    wgu.at[(2 * h + j) * half : (2 * h + j + 1) * half],
                    w_sem.at[1 + 2 * h + j],
                )
            )
    for load in loads:
        load.start()

    line = lax.broadcasted_iota(jnp.int32, (128, n_tok), 0)
    routes = routes_ref[...].astype(F32)
    probs = probs_ref[...].astype(F32)
    table = jnp.where(line == 0, routes[0:1], routes[1:2])
    table = jnp.where(line == 2, probs[0:1], table)
    table = jnp.where(line == 3, probs[1:2], table).T
    lane = lax.broadcasted_iota(jnp.int32, (n_tok, 128), 1)
    place = jnp.zeros((1, 128), jnp.int32)
    for i in range(1, n_shift):
        place = place + jnp.where(lane[0:1] == owner(i), i * CAP, 0)
    earlier = (
        lax.broadcasted_iota(jnp.int32, (n_tok, n_tok), 0)
        > lax.broadcasted_iota(jnp.int32, (n_tok, n_tok), 1)
    )
    earlier = jnp.where(earlier, 1.0, 0.0).astype(BF16)
    slot = lax.broadcasted_iota(jnp.int32, (n_tok, n_shift * CAP), 1)
    offset = place.astype(F32)
    scaled = jnp.zeros((n_tok, n_shift * CAP), F32)
    for k in range(2):
        named = lane == table[:, k : k + 1].astype(jnp.int32)
        hot = jnp.where(named, 1.0, 0.0)
        rank = dot(earlier, hot.astype(BF16), NN) + offset
        offset = offset + jnp.sum(hot, axis=0, keepdims=True)
        target = jnp.sum(jnp.where(named, rank, 0.0), axis=1, keepdims=True)
        chosen = slot == target.astype(jnp.int32)
        pick[k] = jnp.where(chosen, 1.0, 0.0).astype(BF16)
        scaled = scaled + jnp.where(chosen, table[:, 2 + k : 3 + k], 0.0)
    pick_scaled[...] = scaled.astype(BF16)

    for g in range(groups):
        at = slice(g * ROWS, (g + 1) * ROWS)
        both = pick[0, :, at] + pick[1, :, at]
        for c in range(chunks):
            cols = slice(c * COLS, (c + 1) * COLS)
            xs[c, at] = dot(both, tok_ref[:, cols], TN).astype(BF16)
        if g == 0:
            pl.semaphore_wait(barrier, n_shift + 1)
        for c in range(chunks):
            for i in range(max(1, g * GROUP), (g + 1) * GROUP):
                rows = slice(i * CAP, (i + 1) * CAP)
                remote(
                    xs.at[c, rows], xr.at[c, rows], x_s, x_r.at[g], (owner(i), z)
                ).start()
    for c in range(chunks):
        cols = slice(c * COLS, (c + 1) * COLS)
        for g in range(groups):
            at = slice(g * ROWS, (g + 1) * ROWS)
            ss[c, at] = dot(pick_scaled[:, at], dy_ref[:, cols], TN).astype(BF16)
        for j, (block, low, size) in enumerate(PIECES):
            for i in range(1, n_shift) if block == c else ():
                at = (c, slice(i * CAP, (i + 1) * CAP), slice(low, low + size))
                remote(ss.at[at], sr.at[at], s_s, s_r.at[j], (owner(i), z)).start()
    for c in range(chunks):
        xr[c, 0:CAP] = xs[c, 0:CAP]
        sr[c, 0:CAP] = ss[c, 0:CAP]
    for load in loads:
        load.wait()

    for g in range(groups):
        first = CAP if g == 0 else g * ROWS
        took = slice(first, (g + 1) * ROWS)
        remote(xs.at[:, took], xr.at[:, took], x_s, x_r.at[g], (me, z)).wait_recv()
        at = slice(g * ROWS, (g + 1) * ROWS)

        def project(t, _, at=at):
            rows = pl.ds(pl.multiple_of(t * 4 * half, 4 * half), 4 * half)
            pre = jnp.zeros((4 * half, ROWS), F32)
            for c in range(chunks):
                cols = slice(c * COLS, (c + 1) * COLS)
                pre = pre + dot(wgu[rows, cols], xr[c, at], NT)
            for j in range(2):
                gate = pre[2 * j * half : (2 * j + 1) * half]
                upward = pre[(2 * j + 1) * half : (2 * j + 2) * half]
                into = pl.ds(pl.multiple_of((2 * t + j) * half, half), half)
                sig = jax.nn.sigmoid(gate)
                silu = gate * sig
                act[into, at] = (silu * upward).astype(BF16)
                slope[into, at] = upward * (sig + silu * (1.0 - sig))
                silus[into, at] = silu
            return 0

        lax.fori_loop(0, HALVES // 2, project, 0)

    sent = slice(CAP, n_shift * CAP)
    remote(xs.at[:, sent], xr.at[:, sent], x_s, x_r.at[0], (me, z)).wait_send()

    def part_rows(h, size):
        return pl.ds(pl.multiple_of(h * size, size), size)

    def piece(j):
        block, low, size = PIECES[j]
        return block, slice(low, low + size)

    def down_half(h, j):
        block, cols = piece(j)
        return dot(act[part_rows(h, half)], sr[block, :, cols], NN)

    D_ROWS = [slice(k * half, (k + 1) * half) for k in range(6)]

    def down_copy(k, j):
        block, cols = piece(j)
        dst = (far_d.at[0], far_d.at[1], mid_d.at[1], mid_d.at[0], near_d.at[0], near_d.at[1])
        return remote(
            xs.at[block, D_ROWS[k], cols],
            dst[k].at[block, :, cols],
            d_s.at[k, j],
            d_r.at[k, j],
            (me, up if k % 2 == 0 else down),
        )

    halves = (2 * across, 2 * across + 1, 2 * up + 1, 2 * down, 2 * up, 2 * down + 1)

    def down_first(j):
        block, cols = piece(j)
        for k in range(4):
            xs[block, D_ROWS[k], cols] = down_half(halves[k], j).astype(BF16)
            down_copy(k, j).start()
        for part in range(2):
            at = (part * chunks + block) * half
            own_d[at : at + half, cols] = down_half(2 * z + part, j)

    def down_second(j):
        block, cols = piece(j)
        for k in range(4, 6):
            value = down_half(halves[k], j)
            down_copy(k - 4, j).wait_recv()
            value = value + far_d[k - 4, block, :, cols].astype(F32)
            xs[block, D_ROWS[k], cols] = value.astype(BF16)
            down_copy(k, j).start()

    def piece_arrived(j):
        block, cols = piece(j)
        at = (block, sent, cols)
        remote(ss.at[at], sr.at[at], s_s, s_r.at[j], (me, z)).wait_recv()

    def weight_cols(j):
        block, low, size = PIECES[j]
        return slice(block * COLS + low, block * COLS + low + size)

    big = 4 * half
    last = len(PIECES) - 1
    for j in range(last):
        block, cols = piece(j)
        piece_arrived(j)
        down_first(j)

        def project_back(t, _, j=j, block=block, cols=cols):
            rows = part_rows(t, big)
            value = dot(wd[rows, weight_cols(j)], sr[block, :, cols], NT)
            backs[rows] = value if j == 0 else backs[rows] + value
            return 0

        lax.fori_loop(0, HALVES // 4, project_back, 0)
        down_second(j)

    piece_arrived(last)
    remote(ss.at[:, sent], sr.at[:, sent], s_s, s_r.at[0], (me, z)).wait_send()
    last_block, last_cols = piece(last)

    def finish_half(h):
        rows = part_rows(h, half)
        rest = dot(wd[rows, weight_cols(last)], sr[last_block, :, last_cols], NT)
        back = backs[rows] + rest
        dgu[pl.ds(pl.multiple_of(2 * h * half, 2 * half), half)] = (
            back * slope[rows]
        ).astype(BF16)
        dgu[pl.ds(pl.multiple_of((2 * h + 1) * half, half), half)] = (
            back * silus[rows]
        ).astype(BF16)
        return jnp.sum(act[rows].astype(F32) * back, axis=0, keepdims=True)

    def gate_up_half(h, c):
        return dot(dgu[part_rows(h, 2 * half)], xr[c], NN)

    def gate_up_copy(k, c):
        dst = (far_gu.at[0], far_gu.at[1], mid_gu.at[1], mid_gu.at[0], near_gu.at[0], near_gu.at[1])
        size = 2 * half
        if k < 5:
            src = ss.at[c, k * size : (k + 1) * size]
        else:
            src = xs.at[c, 6 * half : 6 * half + size]
        return src, remote(
            src,
            dst[k].at[c],
            gu_s.at[k, c],
            gu_r.at[k, c],
            (me, up if k % 2 == 0 else down),
        )

    def send_gate_up(k, c):
        value = gate_up_half(halves[k], c)
        src, copy = gate_up_copy(k, c)
        if k >= 4:
            gate_up_copy(k - 4, c)[1].wait_recv()
            value = value + far_gu[k - 4, c].astype(F32)
        src[...] = value.astype(BF16)
        copy.start()

    def return_tile(g, n):
        at = slice(g * ROWS, (g + 1) * ROWS)
        cols = pl.ds(pl.multiple_of(n * COLS, COLS), COLS)
        back_s[n, at] = dot(dgu[:, at], wgu[:, cols], TN).astype(BF16)
        for i in range(max(1, g * GROUP), (g + 1) * GROUP):
            rows = slice(i * CAP, (i + 1) * CAP)
            remote(
                back_s.at[n, rows],
                back_r.at[n, rows],
                back_ss,
                back_rs.at[n],
                (source(i), z),
            ).start()

    total = finish_half(halves[0]) + finish_half(halves[1])
    send_gate_up(0, 0)
    send_gate_up(1, 0)
    total = lax.fori_loop(
        2, HALVES, lambda i, t: t + finish_half((2 * across + i) % HALVES), total
    )

    def with_far(n, _):
        return_tile(0, n)

        @pl.when(n < chunks - 1)
        def _():
            send_gate_up(0, n + 1)
            send_gate_up(1, n + 1)

        return 0

    lax.fori_loop(0, chunks, with_far, 0)

    def with_near(n, _):
        return_tile(1, n)
        send_gate_up(2, n)
        send_gate_up(3, n)
        return 0

    lax.fori_loop(0, chunks, with_near, 0)

    high = total.astype(BF16).astype(F32)
    line = lax.broadcasted_iota(jnp.int32, (128, n_shift * CAP), 0)
    pair = jnp.where(line == 0, high, jnp.where(line == 1, total - high, 0.0))
    prob_s[...] = pair.T.astype(BF16)
    for i in range(1, n_shift):
        rows = slice(i * CAP, (i + 1) * CAP)
        remote(
            prob_s.at[rows], prob_r.at[rows], prob_ss, prob_rs, (source(i), z)
        ).start()
    down_first(last)

    def rest_back(n, _):
        return_tile(2, n)
        return_tile(3, n)
        return 0

    lax.fori_loop(0, chunks, rest_back, 0)

    def with_far_sum(c, _):
        send_gate_up(4, c)
        send_gate_up(5, c)
        return 0

    lax.fori_loop(0, chunks, with_far_sum, 0)
    down_second(last)
    for part in range(2):

        def keep(c, _, part=part):
            value = gate_up_half(2 * z + part, c)
            gate_up_copy(3 - part, c)[1].wait_recv()
            value = value + mid_gu[part, c].astype(F32)
            rows = part_rows(part * chunks + c, half)
            slope[rows, 0:COLS] = value[0:half]
            slope[rows, COLS : 2 * COLS] = value[half : 2 * half]
            return 0

        lax.fori_loop(0, chunks, keep, 0)
        for j in range(last + 1):
            down_copy(3 - part, j).wait_recv()
        for c in range(chunks):
            at = slice((part * chunks + c) * half, (part * chunks + c + 1) * half)
            own_d[at] = own_d[at] + mid_d[part, c].astype(F32)
    own = [
        pltpu.make_async_copy(slope, own_gu_hbm, own_sem.at[0]),
        pltpu.make_async_copy(own_d, own_d_hbm, own_sem.at[1]),
    ]
    for copy in own:
        copy.start()

    back_r[:, 0:CAP] = back_s[:, 0:CAP]
    prob_r[0:CAP] = prob_s[0:CAP]
    remote(prob_s.at[sent], prob_r.at[sent], prob_ss, prob_rs, (me, z)).wait_recv()
    for k in range(2):
        terms = dot(pick[k], prob_r[...], NN).T
        dprob_ref[k : k + 1] = (
            jnp.sum(terms, axis=0, keepdims=True) / probs_ref[...].astype(F32)[k : k + 1]
        )

    def combine(n, _):
        remote(
            back_s.at[n, sent], back_r.at[n, sent], back_ss, back_rs.at[n], (me, z)
        ).wait_recv()
        cols = pl.ds(pl.multiple_of(n * COLS, COLS), COLS)
        both = pick[0] + pick[1]
        dtok_ref[:, cols] = dot(both, back_r[n], NN).astype(BF16)
        return 0

    lax.fori_loop(0, chunks, combine, 0)

    for k in range(6):
        for j in range(last + 1):
            if k >= 4:
                down_copy(k, j).wait_recv()
            down_copy(k, j).wait_send()

    def finish(c, _):
        for k in range(6):
            if k >= 4:
                gate_up_copy(k, c)[1].wait_recv()
            gate_up_copy(k, c)[1].wait_send()
        return 0

    lax.fori_loop(0, chunks, finish, 0)
    for copy in own:
        copy.wait()
    remote(
        back_s.at[:, sent], back_r.at[:, sent], back_ss, back_rs.at[0], (me, z)
    ).wait_send()
    remote(prob_s.at[sent], prob_r.at[sent], prob_ss, prob_rs, (me, z)).wait_send()


def add_up(own_gu, own_d, near_gu, near_d, tok_in, prob_in, tok, prob, gg, gu, gd):
    half = gg.shape[0]
    gg[...] = own_gu[:, 0:COLS] + near_gu[0, 0, 0:half].astype(F32)
    gu[...] = own_gu[:, COLS : 2 * COLS] + near_gu[0, 0, half : 2 * half].astype(F32)
    gd[...] = own_d[...] + near_d[0, 0].astype(F32)
    tok[...] = tok_in[...]
    prob[...] = prob_in[...]


def per_device(tokens, grad_out, routes, gate_probs, w_gate, w_up, w_down):
    n_tok, width = tokens.shape
    hidden = w_gate.shape[1]
    half = hidden // HALVES
    slots = len(SHIFTS) * CAP
    chunks = width // COLS
    vmem = pl.BlockSpec(memory_space=pltpu.VMEM)
    hbm = pl.BlockSpec(memory_space=pl.ANY)
    weights = [w[0] for w in (w_gate, w_up, w_down)]
    dma = pltpu.SemaphoreType.DMA
    d_tokens, d_probs, own_gu, own_d, near_gu, near_d = pl.pallas_call(
        kernel,
        out_shape=(
            jax.ShapeDtypeStruct((n_tok, width), BF16),
            jax.ShapeDtypeStruct((2, n_tok), F32),
            jax.ShapeDtypeStruct((hidden, 2 * COLS), F32),
            jax.ShapeDtypeStruct((hidden, COLS), F32),
            jax.ShapeDtypeStruct((2, chunks, 2 * half, COLS), BF16),
            jax.ShapeDtypeStruct((2, chunks, half, COLS), BF16),
        ),
        in_specs=[vmem] * 4 + [hbm] * 3,
        out_specs=[vmem] * 2 + [hbm] * 4,
        scratch_shapes=[
            pltpu.VMEM((2, n_tok, slots), BF16),
            pltpu.VMEM((n_tok, slots), BF16),
            pltpu.VMEM((chunks, slots, COLS), BF16),
            pltpu.VMEM((chunks, slots, COLS), BF16),
            pltpu.VMEM((chunks, slots, COLS), BF16),
            pltpu.VMEM((chunks, slots, COLS), BF16),
            pltpu.VMEM((2 * hidden, width), BF16),
            pltpu.VMEM((hidden, width), BF16),
            pltpu.VMEM((2 * hidden, slots), BF16),
            pltpu.VMEM((hidden, slots), BF16),
            pltpu.VMEM((hidden, slots), F32),
            pltpu.VMEM((hidden, slots), F32),
            pltpu.VMEM((hidden, slots), F32),
            pltpu.VMEM((hidden, COLS), F32),
            pltpu.VMEM((chunks, slots, COLS), BF16),
            pltpu.VMEM((chunks, slots, COLS), BF16),
            pltpu.VMEM((slots, 128), BF16),
            pltpu.VMEM((slots, 128), BF16),
            pltpu.VMEM((2, chunks, 2 * half, COLS), BF16),
            pltpu.VMEM((2, chunks, half, COLS), BF16),
            pltpu.VMEM((2, chunks, 2 * half, COLS), BF16),
            pltpu.VMEM((2, chunks, half, COLS), BF16),
            dma((1 + 2 * HALVES,)),
            dma,
            dma((len(SHIFTS) // GROUP,)),
            dma,
            dma((len(PIECES),)),
            dma,
            dma((chunks,)),
            dma,
            dma,
            dma((6, chunks)),
            dma((6, chunks)),
            dma((6, len(PIECES))),
            dma((6, len(PIECES))),
            dma((2,)),
        ],
        compiler_params=pltpu.CompilerParams(
            collective_id=0, has_side_effects=True, vmem_limit_bytes=63 << 20
        ),
        name="routed_backward",
    )(tokens, grad_out, routes.T, gate_probs.T, *weights)
    step = lambda p, c: (p * chunks + c, 0)
    fixed = lambda p, c: (0, 0)
    tile = pl.BlockSpec((half, COLS), lambda p, c: (p, c))
    rows = pl.BlockSpec((n_tok // HALVES, width), step)
    row_probs = pl.BlockSpec((2, n_tok), fixed)
    shard = jax.ShapeDtypeStruct((hidden // 4, width), F32)
    d_tokens, d_probs, grad_g, grad_u, grad_d = pl.pallas_call(
        add_up,
        grid=(2, chunks),
        out_shape=(
            jax.ShapeDtypeStruct((n_tok, width), BF16),
            jax.ShapeDtypeStruct((2, n_tok), F32),
            shard,
            shard,
            shard,
        ),
        in_specs=[
            pl.BlockSpec((half, 2 * COLS), step),
            pl.BlockSpec((half, COLS), step),
            pl.BlockSpec((1, 1, 2 * half, COLS), lambda p, c: (p, c, 0, 0)),
            pl.BlockSpec((1, 1, half, COLS), lambda p, c: (p, c, 0, 0)),
            rows,
            row_probs,
        ],
        out_specs=[rows, row_probs, tile, tile, tile],
        name="add_up",
    )(own_gu, own_d, near_gu, near_d, d_tokens, d_probs)
    return d_tokens, d_probs.T, grad_g[None], grad_u[None], grad_d[None]


def solution(mesh):
    rows, experts = P(("expert", "dp"), None), P("expert", None, None)
    split = P("expert", "dp", None)
    return jax.shard_map(
        per_device,
        mesh=mesh,
        in_specs=(rows, rows, rows, rows, experts, experts, experts),
        out_specs=(rows, rows, split, split, split),
        check_vma=False,
    )
```

```python
import functools

import jax
import jax.numpy as jnp
from jax import lax
from jax.experimental import pallas as pl
from jax.experimental.pallas import tpu as pltpu
from jax.sharding import PartitionSpec as P

F32 = jnp.float32
BF16 = jnp.bfloat16
MESH = pl.DeviceIdType.MESH
NT = (((1,), (1,)), ((), ()))
TN = (((0,), (0,)), ((), ()))
NN = (((1,), (0,)), ((), ()))

RINGS = (
    ((2, 0), (0, 2), (2, 2)),
    ((2, 1), (1, 2), (2, 3), (3, 2)),
    ((1, 1), (3, 3), (1, 3), (3, 1)),
    ((1, 0), (0, 1), (3, 0), (0, 3)),
)
SHIFTS = [(0, 0, 0), (0, 0, 1)] + [
    (dx, dy, dc) for ring in RINGS for dc in (0, 1) for dx, dy in ring
]
CAP = 32
GROUP = 8
ROWS = GROUP * CAP
COLS = 512
PIECES = ((0, 0, 512), (1, 0, 512), (2, 0, 512), (3, 0, 256), (3, 256, 256))
HALVES = 8


def dot(a, b, dims):
    return lax.dot_general(a, b, dims, preferred_element_type=F32)


def kernel(
    tok_ref,
    dy_hbm,
    routes_ref,
    probs_ref,
    wg_hbm,
    wu_hbm,
    wd_hbm,
    dtok_hbm,
    dprob_ref,
    own_gu_hbm,
    own_d_hbm,
    near_gu,
    near_d,
    dy_ref,
    dtok_ref,
    pick,
    pick_scaled,
    xs,
    ss,
    xr,
    sr,
    wgu,
    wd,
    dgu,
    act,
    slope,
    silus,
    backs,
    own_d,
    back_s,
    back_r,
    prob_s,
    prob_r,
    far_gu,
    far_d,
    mid_gu,
    mid_d,
    w_sem,
    x_s,
    x_r,
    s_s,
    s_r,
    back_ss,
    back_rs,
    prob_ss,
    prob_rs,
    gu_s,
    gu_r,
    d_s,
    d_r,
    own_sem,
    dy_sem,
    dtok_sem,
):
    me, z = lax.axis_index("expert"), lax.axis_index("dp")
    cx, cy, core = me // 8, (me // 2) % 4, me % 2
    up, down, across = (z + 1) % 4, (z + 3) % 4, (z + 2) % 4
    n_shift = len(SHIFTS)
    groups = n_shift // GROUP
    n_tok, width = tok_ref.shape
    chunks = width // COLS
    half = wd.shape[0] // HALVES

    def owner(i):
        dx, dy, dc = SHIFTS[i]
        return ((cx + dx) % 4) * 8 + ((cy + dy) % 4) * 2 + (core + dc) % 2

    def source(i):
        dx, dy, dc = SHIFTS[i]
        return ((cx + 4 - dx) % 4) * 8 + ((cy + 4 - dy) % 4) * 2 + (core + dc) % 2

    def remote(src, dst, send_sem, recv_sem, device):
        return pltpu.make_async_remote_copy(
            src_ref=src,
            dst_ref=dst,
            send_sem=send_sem,
            recv_sem=recv_sem,
            device_id=device,
            device_id_type=MESH,
        )

    barrier = pltpu.get_barrier_semaphore()
    for i in range(1, n_shift):
        pl.semaphore_signal(barrier, inc=1, device_id=(owner(i), z), device_id_type=MESH)
    for other in (up, down):
        pl.semaphore_signal(barrier, inc=1, device_id=(me, other), device_id_type=MESH)

    dy_load = pltpu.make_async_copy(dy_hbm, dy_ref, dy_sem)
    dy_load.start()
    loads = [
        pltpu.make_async_copy(wd_hbm, wd, w_sem.at[0]),
    ]
    for h in range(HALVES):
        for j, w in enumerate((wg_hbm, wu_hbm)):
            loads.append(
                pltpu.make_async_copy(
                    w.at[h * half : (h + 1) * half],
                    wgu.at[(2 * h + j) * half : (2 * h + j + 1) * half],
                    w_sem.at[1 + 2 * h + j],
                )
            )
    for load in loads:
        load.start()

    line = lax.broadcasted_iota(jnp.int32, (128, n_tok), 0)
    routes = routes_ref[...].astype(F32)
    probs = probs_ref[...].astype(F32)
    table = jnp.where(line == 0, routes[0:1], routes[1:2])
    table = jnp.where(line == 2, probs[0:1], table)
    table = jnp.where(line == 3, probs[1:2], table).T
    lane = lax.broadcasted_iota(jnp.int32, (n_tok, 128), 1)
    place = jnp.zeros((1, 128), jnp.int32)
    for i in range(1, n_shift):
        place = place + jnp.where(lane[0:1] == owner(i), i * CAP, 0)
    earlier = (
        lax.broadcasted_iota(jnp.int32, (n_tok, n_tok), 0)
        > lax.broadcasted_iota(jnp.int32, (n_tok, n_tok), 1)
    )
    earlier = jnp.where(earlier, 1.0, 0.0).astype(BF16)
    slot = lax.broadcasted_iota(jnp.int32, (n_tok, ROWS), 1)
    offset = place.astype(F32)
    targets = []
    for k in range(2):
        named = lane == table[:, k : k + 1].astype(jnp.int32)
        hot = jnp.where(named, 1.0, 0.0)
        rank = dot(earlier, hot.astype(BF16), NN) + offset
        offset = offset + jnp.sum(hot, axis=0, keepdims=True)
        target = jnp.sum(jnp.where(named, rank, 0.0), axis=1, keepdims=True)
        targets.append(target.astype(jnp.int32))

    for g in range(groups):
        at = slice(g * ROWS, (g + 1) * ROWS)
        chosen = [slot == target - g * ROWS for target in targets]
        both = jnp.where(chosen[0] | chosen[1], 1.0, 0.0).astype(BF16)
        for c in range(chunks):
            cols = slice(c * COLS, (c + 1) * COLS)
            xs[c, at] = dot(both, tok_ref[:, cols], TN).astype(BF16)
            if g == 0 and c == 0:
                pl.semaphore_wait(barrier, n_shift + 1)
            for i in range(max(1, g * GROUP), (g + 1) * GROUP):
                rows = slice(i * CAP, (i + 1) * CAP)
                remote(
                    xs.at[c, rows], xr.at[c, rows], x_s, x_r.at[g], (owner(i), z)
                ).start()
        scaled = jnp.zeros((n_tok, ROWS), F32)
        for k in range(2):
            pick[k, :, at] = jnp.where(chosen[k], 1.0, 0.0).astype(BF16)
            scaled = scaled + jnp.where(chosen[k], table[:, 2 + k : 3 + k], 0.0)
        pick_scaled[:, at] = scaled.astype(BF16)
    dy_load.wait()
    for c in range(chunks):
        cols = slice(c * COLS, (c + 1) * COLS)
        for g in range(groups):
            at = slice(g * ROWS, (g + 1) * ROWS)
            ss[c, at] = dot(pick_scaled[:, at], dy_ref[:, cols], TN).astype(BF16)
        for j, (block, low, size) in enumerate(PIECES):
            for i in range(1, n_shift) if block == c else ():
                at = (c, slice(i * CAP, (i + 1) * CAP), slice(low, low + size))
                remote(ss.at[at], sr.at[at], s_s, s_r.at[j], (owner(i), z)).start()
    for c in range(chunks):
        xr[c, 0:CAP] = xs[c, 0:CAP]
        sr[c, 0:CAP] = ss[c, 0:CAP]
    for load in loads:
        load.wait()

    for g in range(groups):
        first = CAP if g == 0 else g * ROWS
        took = slice(first, (g + 1) * ROWS)
        remote(xs.at[:, took], xr.at[:, took], x_s, x_r.at[g], (me, z)).wait_recv()
        at = slice(g * ROWS, (g + 1) * ROWS)

        def project(t, _, at=at):
            rows = pl.ds(pl.multiple_of(t * 4 * half, 4 * half), 4 * half)
            pre = jnp.zeros((4 * half, ROWS), F32)
            for c in range(chunks):
                cols = slice(c * COLS, (c + 1) * COLS)
                pre = pre + dot(wgu[rows, cols], xr[c, at], NT)
            for j in range(2):
                gate = pre[2 * j * half : (2 * j + 1) * half]
                upward = pre[(2 * j + 1) * half : (2 * j + 2) * half]
                into = pl.ds(pl.multiple_of((2 * t + j) * half, half), half)
                sig = jax.nn.sigmoid(gate)
                silu = gate * sig
                act[into, at] = (silu * upward).astype(BF16)
                slope[into, at] = upward * (sig + silu * (1.0 - sig))
                silus[into, at] = silu
            return 0

        lax.fori_loop(0, HALVES // 2, project, 0)

    sent = slice(CAP, n_shift * CAP)
    remote(xs.at[:, sent], xr.at[:, sent], x_s, x_r.at[0], (me, z)).wait_send()

    def part_rows(h, size):
        return pl.ds(pl.multiple_of(h * size, size), size)

    def piece(j):
        block, low, size = PIECES[j]
        return block, slice(low, low + size)

    def down_half(h, j):
        block, cols = piece(j)
        return dot(act[part_rows(h, half)], sr[block, :, cols], NN)

    D_ROWS = [slice(k * half, (k + 1) * half) for k in range(6)]

    def down_copy(k, j):
        block, cols = piece(j)
        dst = (far_d.at[0], far_d.at[1], mid_d.at[1], mid_d.at[0], near_d.at[0], near_d.at[1])
        return remote(
            xs.at[block, D_ROWS[k], cols],
            dst[k].at[block, :, cols],
            d_s.at[k, j],
            d_r.at[k, j],
            (me, up if k % 2 == 0 else down),
        )

    halves = (2 * across, 2 * across + 1, 2 * up + 1, 2 * down, 2 * up, 2 * down + 1)

    def down_first(j):
        block, cols = piece(j)
        for k in range(4):
            xs[block, D_ROWS[k], cols] = down_half(halves[k], j).astype(BF16)
            down_copy(k, j).start()
        for part in range(2):
            at = (part * chunks + block) * half
            own_d[at : at + half, cols] = down_half(2 * z + part, j)

    def down_second(j):
        block, cols = piece(j)
        for k in range(4, 6):
            value = down_half(halves[k], j)
            down_copy(k - 4, j).wait_recv()
            value = value + far_d[k - 4, block, :, cols].astype(F32)
            xs[block, D_ROWS[k], cols] = value.astype(BF16)
            down_copy(k, j).start()

    def piece_arrived(j):
        block, cols = piece(j)
        at = (block, sent, cols)
        remote(ss.at[at], sr.at[at], s_s, s_r.at[j], (me, z)).wait_recv()

    def weight_cols(j):
        block, low, size = PIECES[j]
        return slice(block * COLS + low, block * COLS + low + size)

    big = 4 * half
    last = len(PIECES) - 1
    for j in range(last):
        block, cols = piece(j)
        piece_arrived(j)
        down_first(j)

        def project_back(t, _, j=j, block=block, cols=cols):
            rows = part_rows(t, big)
            value = dot(wd[rows, weight_cols(j)], sr[block, :, cols], NT)
            backs[rows] = value if j == 0 else backs[rows] + value
            return 0

        lax.fori_loop(0, HALVES // 4, project_back, 0)
        down_second(j)

    piece_arrived(last)
    remote(ss.at[:, sent], sr.at[:, sent], s_s, s_r.at[0], (me, z)).wait_send()
    last_block, last_cols = piece(last)

    def finish_half(h):
        rows = part_rows(h, half)
        rest = dot(wd[rows, weight_cols(last)], sr[last_block, :, last_cols], NT)
        back = backs[rows] + rest
        dgu[pl.ds(pl.multiple_of(2 * h * half, 2 * half), half)] = (
            back * slope[rows]
        ).astype(BF16)
        dgu[pl.ds(pl.multiple_of((2 * h + 1) * half, half), half)] = (
            back * silus[rows]
        ).astype(BF16)
        return jnp.sum(act[rows].astype(F32) * back, axis=0, keepdims=True)

    def gate_up_half(h, c):
        return dot(dgu[part_rows(h, 2 * half)], xr[c], NN)

    def gate_up_copy(k, c):
        dst = (far_gu.at[0], far_gu.at[1], mid_gu.at[1], mid_gu.at[0], near_gu.at[0], near_gu.at[1])
        size = 2 * half
        if k < 5:
            src = ss.at[c, k * size : (k + 1) * size]
        else:
            src = xs.at[c, 6 * half : 6 * half + size]
        return src, remote(
            src,
            dst[k].at[c],
            gu_s.at[k, c],
            gu_r.at[k, c],
            (me, up if k % 2 == 0 else down),
        )

    def send_gate_up(k, c):
        value = gate_up_half(halves[k], c)
        src, copy = gate_up_copy(k, c)
        if k >= 4:
            gate_up_copy(k - 4, c)[1].wait_recv()
            value = value + far_gu[k - 4, c].astype(F32)
        src[...] = value.astype(BF16)
        copy.start()

    def return_tile(g, n):
        at = slice(g * ROWS, (g + 1) * ROWS)
        cols = pl.ds(pl.multiple_of(n * COLS, COLS), COLS)
        back_s[n, at] = dot(dgu[:, at], wgu[:, cols], TN).astype(BF16)
        for i in range(max(1, g * GROUP), (g + 1) * GROUP):
            rows = slice(i * CAP, (i + 1) * CAP)
            remote(
                back_s.at[n, rows],
                back_r.at[n, rows],
                back_ss,
                back_rs.at[n],
                (source(i), z),
            ).start()

    total = finish_half(halves[0]) + finish_half(halves[1])
    send_gate_up(0, 0)
    send_gate_up(1, 0)
    total = lax.fori_loop(
        2, HALVES, lambda i, t: t + finish_half((2 * across + i) % HALVES), total
    )

    def with_far(n, _):
        return_tile(0, n)

        @pl.when(n < chunks - 1)
        def _():
            send_gate_up(0, n + 1)
            send_gate_up(1, n + 1)

        return 0

    lax.fori_loop(0, chunks, with_far, 0)

    def with_near(n, _):
        return_tile(1, n)
        send_gate_up(2, n)
        send_gate_up(3, n)
        return 0

    lax.fori_loop(0, chunks, with_near, 0)

    high = total.astype(BF16).astype(F32)
    line = lax.broadcasted_iota(jnp.int32, (128, n_shift * CAP), 0)
    pair = jnp.where(line == 0, high, jnp.where(line == 1, total - high, 0.0))
    prob_s[...] = pair.T.astype(BF16)
    for i in range(1, n_shift):
        rows = slice(i * CAP, (i + 1) * CAP)
        remote(
            prob_s.at[rows], prob_r.at[rows], prob_ss, prob_rs, (source(i), z)
        ).start()
    down_first(last)

    def rest_back(n, _):
        return_tile(2, n)
        return_tile(3, n)
        return 0

    lax.fori_loop(0, chunks, rest_back, 0)

    def with_far_sum(c, _):
        send_gate_up(4, c)
        send_gate_up(5, c)
        return 0

    lax.fori_loop(0, chunks, with_far_sum, 0)
    down_second(last)
    for part in range(2):

        def keep(c, _, part=part):
            value = gate_up_half(2 * z + part, c)
            gate_up_copy(3 - part, c)[1].wait_recv()
            value = value + mid_gu[part, c].astype(F32)
            rows = part_rows(part * chunks + c, half)
            slope[rows, 0:COLS] = value[0:half]
            slope[rows, COLS : 2 * COLS] = value[half : 2 * half]
            return 0

        lax.fori_loop(0, chunks, keep, 0)
        for j in range(last + 1):
            down_copy(3 - part, j).wait_recv()
        for c in range(chunks):
            at = slice((part * chunks + c) * half, (part * chunks + c + 1) * half)
            own_d[at] = own_d[at] + mid_d[part, c].astype(F32)
    own = [
        pltpu.make_async_copy(slope, own_gu_hbm, own_sem.at[0]),
        pltpu.make_async_copy(own_d, own_d_hbm, own_sem.at[1]),
    ]
    for copy in own:
        copy.start()

    back_r[:, 0:CAP] = back_s[:, 0:CAP]
    prob_r[0:CAP] = prob_s[0:CAP]
    remote(prob_s.at[sent], prob_r.at[sent], prob_ss, prob_rs, (me, z)).wait_recv()
    for k in range(2):
        terms = dot(pick[k], prob_r[...], NN).T
        dprob_ref[k : k + 1] = (
            jnp.sum(terms, axis=0, keepdims=True) / probs_ref[...].astype(F32)[k : k + 1]
        )

    def token_copy(n):
        cols = pl.ds(pl.multiple_of(n * COLS, COLS), COLS)
        return pltpu.make_async_copy(dtok_ref.at[n], dtok_hbm.at[:, cols], dtok_sem.at[n])

    def combine(n, _):
        remote(
            back_s.at[n, sent], back_r.at[n, sent], back_ss, back_rs.at[n], (me, z)
        ).wait_recv()
        both = pick[0] + pick[1]
        dtok_ref[n] = dot(both, back_r[n], NN).astype(BF16)
        token_copy(n).start()
        return 0

    lax.fori_loop(0, chunks, combine, 0)

    for k in range(6):
        for j in range(last + 1):
            if k >= 4:
                down_copy(k, j).wait_recv()
            down_copy(k, j).wait_send()

    def finish(c, _):
        token_copy(c).wait()
        for k in range(6):
            if k >= 4:
                gate_up_copy(k, c)[1].wait_recv()
            gate_up_copy(k, c)[1].wait_send()
        return 0

    lax.fori_loop(0, chunks, finish, 0)
    for copy in own:
        copy.wait()
    remote(
        back_s.at[:, sent], back_r.at[:, sent], back_ss, back_rs.at[0], (me, z)
    ).wait_send()
    remote(prob_s.at[sent], prob_r.at[sent], prob_ss, prob_rs, (me, z)).wait_send()


def add_up(
    own_gu_hbm,
    own_d_hbm,
    near_gu_hbm,
    near_d_hbm,
    tok_in,
    prob_in,
    tok_out,
    prob_out,
    gg_hbm,
    gu_hbm,
    gd_hbm,
    own_gu,
    own_d,
    near_gu,
    near_d,
    sums,
    in_sem,
    out_sem,
    tok_sem,
):
    half = own_gu.shape[1]
    tiles = own_gu.shape[0]
    chunks = tiles // 2
    pairs = (
        (own_gu_hbm, own_gu),
        (own_d_hbm, own_d),
        (near_gu_hbm, near_gu),
        (near_d_hbm, near_d),
    )
    loads = []
    for t in range(tiles):
        rows = slice(t * half, (t + 1) * half)
        for j, (src, dst) in enumerate(pairs):
            part = src.at[rows] if j < 2 else src.at[t // chunks, t % chunks]
            loads.append(pltpu.make_async_copy(part, dst.at[t], in_sem.at[t, j]))
    for load in loads:
        load.start()
    tok = pltpu.make_async_copy(tok_in, tok_out, tok_sem)
    tok.start()
    prob_out[...] = prob_in[...]
    stores = []
    for t in range(tiles):
        for load in loads[4 * t : 4 * t + 4]:
            load.wait()
        sums[t, 0] = own_gu[t, :, 0:COLS] + near_gu[t, 0:half].astype(F32)
        sums[t, 1] = own_gu[t, :, COLS : 2 * COLS] + near_gu[t, half : 2 * half].astype(F32)
        sums[t, 2] = own_d[t] + near_d[t].astype(F32)
        low = slice((t // chunks) * half, (t // chunks + 1) * half)
        cols = slice((t % chunks) * COLS, (t % chunks + 1) * COLS)
        for j, out in enumerate((gg_hbm, gu_hbm, gd_hbm)):
            store = pltpu.make_async_copy(sums.at[t, j], out.at[low, cols], out_sem.at[t, j])
            store.start()
            stores.append(store)
    for store in stores:
        store.wait()
    tok.wait()


def per_device(tokens, grad_out, routes, gate_probs, w_gate, w_up, w_down):
    n_tok, width = tokens.shape
    hidden = w_gate.shape[1]
    half = hidden // HALVES
    slots = len(SHIFTS) * CAP
    chunks = width // COLS
    vmem = pl.BlockSpec(memory_space=pltpu.VMEM)
    hbm = pl.BlockSpec(memory_space=pl.ANY)
    weights = [w[0] for w in (w_gate, w_up, w_down)]
    dma = pltpu.SemaphoreType.DMA
    d_tokens, d_probs, own_gu, own_d, near_gu, near_d = pl.pallas_call(
        kernel,
        out_shape=(
            jax.ShapeDtypeStruct((n_tok, width), BF16),
            jax.ShapeDtypeStruct((2, n_tok), F32),
            jax.ShapeDtypeStruct((hidden, 2 * COLS), F32),
            jax.ShapeDtypeStruct((hidden, COLS), F32),
            jax.ShapeDtypeStruct((2, chunks, 2 * half, COLS), BF16),
            jax.ShapeDtypeStruct((2, chunks, half, COLS), BF16),
        ),
        in_specs=[vmem, hbm, vmem, vmem] + [hbm] * 3,
        out_specs=[hbm, vmem] + [hbm] * 4,
        scratch_shapes=[
            pltpu.VMEM((n_tok, width), BF16),
            pltpu.VMEM((chunks, n_tok, COLS), BF16),
            pltpu.VMEM((2, n_tok, slots), BF16),
            pltpu.VMEM((n_tok, slots), BF16),
            pltpu.VMEM((chunks, slots, COLS), BF16),
            pltpu.VMEM((chunks, slots, COLS), BF16),
            pltpu.VMEM((chunks, slots, COLS), BF16),
            pltpu.VMEM((chunks, slots, COLS), BF16),
            pltpu.VMEM((2 * hidden, width), BF16),
            pltpu.VMEM((hidden, width), BF16),
            pltpu.VMEM((2 * hidden, slots), BF16),
            pltpu.VMEM((hidden, slots), BF16),
            pltpu.VMEM((hidden, slots), F32),
            pltpu.VMEM((hidden, slots), F32),
            pltpu.VMEM((hidden, slots), F32),
            pltpu.VMEM((hidden, COLS), F32),
            pltpu.VMEM((chunks, slots, COLS), BF16),
            pltpu.VMEM((chunks, slots, COLS), BF16),
            pltpu.VMEM((slots, 128), BF16),
            pltpu.VMEM((slots, 128), BF16),
            pltpu.VMEM((2, chunks, 2 * half, COLS), BF16),
            pltpu.VMEM((2, chunks, half, COLS), BF16),
            pltpu.VMEM((2, chunks, 2 * half, COLS), BF16),
            pltpu.VMEM((2, chunks, half, COLS), BF16),
            dma((1 + 2 * HALVES,)),
            dma,
            dma((len(SHIFTS) // GROUP,)),
            dma,
            dma((len(PIECES),)),
            dma,
            dma((chunks,)),
            dma,
            dma,
            dma((6, chunks)),
            dma((6, chunks)),
            dma((6, len(PIECES))),
            dma((6, len(PIECES))),
            dma((2,)),
            dma,
            dma((chunks,)),
        ],
        compiler_params=pltpu.CompilerParams(
            collective_id=0, has_side_effects=True, vmem_limit_bytes=63 << 20
        ),
        name="routed_backward",
    )(tokens, grad_out, routes.T, gate_probs.T, *weights)
    tiles = 2 * chunks
    shard = jax.ShapeDtypeStruct((hidden // 4, width), F32)
    d_tokens, d_probs, grad_g, grad_u, grad_d = pl.pallas_call(
        add_up,
        out_shape=(
            jax.ShapeDtypeStruct((n_tok, width), BF16),
            jax.ShapeDtypeStruct((2, n_tok), F32),
            shard,
            shard,
            shard,
        ),
        in_specs=[hbm] * 5 + [vmem],
        out_specs=[hbm, vmem] + [hbm] * 3,
        scratch_shapes=[
            pltpu.VMEM((tiles, half, 2 * COLS), F32),
            pltpu.VMEM((tiles, half, COLS), F32),
            pltpu.VMEM((tiles, 2 * half, COLS), BF16),
            pltpu.VMEM((tiles, half, COLS), BF16),
            pltpu.VMEM((tiles, 3, half, COLS), F32),
            dma((tiles, 4)),
            dma((tiles, 3)),
            dma,
        ],
        compiler_params=pltpu.CompilerParams(vmem_limit_bytes=62 << 20),
        name="add_up",
    )(own_gu, own_d, near_gu, near_d, d_tokens, d_probs)
    return d_tokens, d_probs.T, grad_g[None], grad_u[None], grad_d[None]


def solution(mesh):
    rows, experts = P(("expert", "dp"), None), P("expert", None, None)
    split = P("expert", "dp", None)
    return jax.shard_map(
        per_device,
        mesh=mesh,
        in_specs=(rows, rows, rows, rows, experts, experts, experts),
        out_specs=(rows, rows, split, split, split),
        check_vma=False,
    )
```

```python
import functools

import jax
import jax.numpy as jnp
from jax import lax
from jax.experimental import pallas as pl
from jax.experimental.pallas import tpu as pltpu
from jax.sharding import PartitionSpec as P

F32 = jnp.float32
BF16 = jnp.bfloat16
MESH = pl.DeviceIdType.MESH
NT = (((1,), (1,)), ((), ()))
TN = (((0,), (0,)), ((), ()))
NN = (((1,), (0,)), ((), ()))

RINGS = (
    ((2, 0), (0, 2), (2, 2)),
    ((2, 1), (1, 2), (2, 3), (3, 2)),
    ((1, 1), (3, 3), (1, 3), (3, 1)),
    ((1, 0), (0, 1), (3, 0), (0, 3)),
)
SHIFTS = [(0, 0, 0), (0, 0, 1)] + [
    (dx, dy, dc) for ring in RINGS for dc in (0, 1) for dx, dy in ring
]
CAP = 32
GROUP = 8
ROWS = GROUP * CAP
COLS = 512
PIECES = ((0, 0, 512), (1, 0, 512), (2, 0, 512), (3, 0, 256), (3, 256, 256))
HALVES = 8


def dot(a, b, dims):
    return lax.dot_general(a, b, dims, preferred_element_type=F32)


def kernel(
    tok_ref,
    dy_hbm,
    routes_ref,
    probs_ref,
    wg_hbm,
    wu_hbm,
    wd_hbm,
    dtok_hbm,
    dprob_ref,
    sum_gu_hbm,
    sum_d_hbm,
    dy_ref,
    dtok_ref,
    pick,
    pick_scaled,
    xs,
    ss,
    xr,
    sr,
    wgu,
    wd,
    dgu,
    act,
    slope,
    silus,
    backs,
    own_d,
    back_s,
    back_r,
    prob_s,
    prob_r,
    far_gu,
    far_d,
    mid_gu,
    mid_d,
    near_gu,
    near_d,
    w_sem,
    x_s,
    x_r,
    s_s,
    s_r,
    back_ss,
    back_rs,
    prob_ss,
    prob_rs,
    gu_s,
    gu_r,
    d_s,
    d_r,
    sum_sem,
    dy_sem,
    dtok_sem,
):
    me, z = lax.axis_index("expert"), lax.axis_index("dp")
    cx, cy, core = me // 8, (me // 2) % 4, me % 2
    up, down, across = (z + 1) % 4, (z + 3) % 4, (z + 2) % 4
    n_shift = len(SHIFTS)
    groups = n_shift // GROUP
    n_tok, width = tok_ref.shape
    chunks = width // COLS
    half = wd.shape[0] // HALVES

    def owner(i):
        dx, dy, dc = SHIFTS[i]
        return ((cx + dx) % 4) * 8 + ((cy + dy) % 4) * 2 + (core + dc) % 2

    def source(i):
        dx, dy, dc = SHIFTS[i]
        return ((cx + 4 - dx) % 4) * 8 + ((cy + 4 - dy) % 4) * 2 + (core + dc) % 2

    def remote(src, dst, send_sem, recv_sem, device):
        return pltpu.make_async_remote_copy(
            src_ref=src,
            dst_ref=dst,
            send_sem=send_sem,
            recv_sem=recv_sem,
            device_id=device,
            device_id_type=MESH,
        )

    barrier = pltpu.get_barrier_semaphore()
    for i in range(1, n_shift):
        pl.semaphore_signal(barrier, inc=1, device_id=(owner(i), z), device_id_type=MESH)
    for other in (up, down):
        pl.semaphore_signal(barrier, inc=1, device_id=(me, other), device_id_type=MESH)

    dy_load = pltpu.make_async_copy(dy_hbm, dy_ref, dy_sem)
    dy_load.start()
    loads = [
        pltpu.make_async_copy(wd_hbm, wd, w_sem.at[0]),
    ]
    for h in range(HALVES):
        for j, w in enumerate((wg_hbm, wu_hbm)):
            loads.append(
                pltpu.make_async_copy(
                    w.at[h * half : (h + 1) * half],
                    wgu.at[(2 * h + j) * half : (2 * h + j + 1) * half],
                    w_sem.at[1 + 2 * h + j],
                )
            )
    for load in loads:
        load.start()

    line = lax.broadcasted_iota(jnp.int32, (128, n_tok), 0)
    routes = routes_ref[...].astype(F32)
    probs = probs_ref[...].astype(F32)
    table = jnp.where(line == 0, routes[0:1], routes[1:2])
    table = jnp.where(line == 2, probs[0:1], table)
    table = jnp.where(line == 3, probs[1:2], table).T
    lane = lax.broadcasted_iota(jnp.int32, (n_tok, 128), 1)
    place = jnp.zeros((1, 128), jnp.int32)
    for i in range(1, n_shift):
        place = place + jnp.where(lane[0:1] == owner(i), i * CAP, 0)
    earlier = (
        lax.broadcasted_iota(jnp.int32, (n_tok, n_tok), 0)
        > lax.broadcasted_iota(jnp.int32, (n_tok, n_tok), 1)
    )
    earlier = jnp.where(earlier, 1.0, 0.0).astype(BF16)
    slot = lax.broadcasted_iota(jnp.int32, (n_tok, ROWS), 1)
    offset = place.astype(F32)
    targets = []
    for k in range(2):
        named = lane == table[:, k : k + 1].astype(jnp.int32)
        hot = jnp.where(named, 1.0, 0.0)
        rank = dot(earlier, hot.astype(BF16), NN) + offset
        offset = offset + jnp.sum(hot, axis=0, keepdims=True)
        target = jnp.sum(jnp.where(named, rank, 0.0), axis=1, keepdims=True)
        targets.append(target.astype(jnp.int32))

    for g in range(groups):
        at = slice(g * ROWS, (g + 1) * ROWS)
        chosen = [slot == target - g * ROWS for target in targets]
        both = jnp.where(chosen[0] | chosen[1], 1.0, 0.0).astype(BF16)
        for c in range(chunks):
            cols = slice(c * COLS, (c + 1) * COLS)
            xs[c, at] = dot(both, tok_ref[:, cols], TN).astype(BF16)
            if g == 0 and c == 0:
                pl.semaphore_wait(barrier, n_shift + 1)
            for i in range(max(1, g * GROUP), (g + 1) * GROUP):
                rows = slice(i * CAP, (i + 1) * CAP)
                remote(
                    xs.at[c, rows], xr.at[c, rows], x_s, x_r.at[g], (owner(i), z)
                ).start()
        scaled = jnp.zeros((n_tok, ROWS), F32)
        for k in range(2):
            pick[k, :, at] = jnp.where(chosen[k], 1.0, 0.0).astype(BF16)
            scaled = scaled + jnp.where(chosen[k], table[:, 2 + k : 3 + k], 0.0)
        pick_scaled[:, at] = scaled.astype(BF16)
    dy_load.wait()
    for c in range(chunks):
        cols = slice(c * COLS, (c + 1) * COLS)
        for g in range(groups):
            at = slice(g * ROWS, (g + 1) * ROWS)
            ss[c, at] = dot(pick_scaled[:, at], dy_ref[:, cols], TN).astype(BF16)
        for j, (block, low, size) in enumerate(PIECES):
            for i in range(1, n_shift) if block == c else ():
                at = (c, slice(i * CAP, (i + 1) * CAP), slice(low, low + size))
                remote(ss.at[at], sr.at[at], s_s, s_r.at[j], (owner(i), z)).start()
    for c in range(chunks):
        xr[c, 0:CAP] = xs[c, 0:CAP]
        sr[c, 0:CAP] = ss[c, 0:CAP]
    for load in loads:
        load.wait()

    for g in range(groups):
        first = CAP if g == 0 else g * ROWS
        took = slice(first, (g + 1) * ROWS)
        remote(xs.at[:, took], xr.at[:, took], x_s, x_r.at[g], (me, z)).wait_recv()
        at = slice(g * ROWS, (g + 1) * ROWS)

        def project(t, _, at=at):
            rows = pl.ds(pl.multiple_of(t * 4 * half, 4 * half), 4 * half)
            pre = jnp.zeros((4 * half, ROWS), F32)
            for c in range(chunks):
                cols = slice(c * COLS, (c + 1) * COLS)
                pre = pre + dot(wgu[rows, cols], xr[c, at], NT)
            for j in range(2):
                gate = pre[2 * j * half : (2 * j + 1) * half]
                upward = pre[(2 * j + 1) * half : (2 * j + 2) * half]
                into = pl.ds(pl.multiple_of((2 * t + j) * half, half), half)
                sig = jax.nn.sigmoid(gate)
                silu = gate * sig
                act[into, at] = (silu * upward).astype(BF16)
                slope[into, at] = upward * (sig + silu * (1.0 - sig))
                silus[into, at] = silu
            return 0

        lax.fori_loop(0, HALVES // 2, project, 0)

    sent = slice(CAP, n_shift * CAP)
    remote(xs.at[:, sent], xr.at[:, sent], x_s, x_r.at[0], (me, z)).wait_send()

    def part_rows(h, size):
        return pl.ds(pl.multiple_of(h * size, size), size)

    def piece(j):
        block, low, size = PIECES[j]
        return block, slice(low, low + size)

    def down_half(h, j):
        block, cols = piece(j)
        return dot(act[part_rows(h, half)], sr[block, :, cols], NN)

    D_ROWS = [slice(k * half, (k + 1) * half) for k in range(6)]

    def down_copy(k, j):
        block, cols = piece(j)
        dst = (far_d.at[0], far_d.at[1], mid_d.at[1], mid_d.at[0], near_d.at[0], near_d.at[1])
        return remote(
            xs.at[block, D_ROWS[k], cols],
            dst[k].at[block, :, cols],
            d_s.at[k, j],
            d_r.at[k, j],
            (me, up if k % 2 == 0 else down),
        )

    halves = (2 * across, 2 * across + 1, 2 * up + 1, 2 * down, 2 * up, 2 * down + 1)

    def down_first(j):
        block, cols = piece(j)
        for k in range(4):
            xs[block, D_ROWS[k], cols] = down_half(halves[k], j).astype(BF16)
            down_copy(k, j).start()
        for part in range(2):
            at = (part * chunks + block) * half
            own_d[at : at + half, cols] = down_half(2 * z + part, j)

    def down_second(j):
        block, cols = piece(j)
        for k in range(4, 6):
            value = down_half(halves[k], j)
            down_copy(k - 4, j).wait_recv()
            value = value + far_d[k - 4, block, :, cols].astype(F32)
            xs[block, D_ROWS[k], cols] = value.astype(BF16)
            down_copy(k, j).start()

    def piece_arrived(j):
        block, cols = piece(j)
        at = (block, sent, cols)
        remote(ss.at[at], sr.at[at], s_s, s_r.at[j], (me, z)).wait_recv()

    def weight_cols(j):
        block, low, size = PIECES[j]
        return slice(block * COLS + low, block * COLS + low + size)

    big = 4 * half
    last = len(PIECES) - 1
    for j in range(last):
        block, cols = piece(j)
        piece_arrived(j)
        down_first(j)

        def project_back(t, _, j=j, block=block, cols=cols):
            rows = part_rows(t, big)
            value = dot(wd[rows, weight_cols(j)], sr[block, :, cols], NT)
            backs[rows] = value if j == 0 else backs[rows] + value
            return 0

        lax.fori_loop(0, HALVES // 4, project_back, 0)
        down_second(j)

    piece_arrived(last)
    remote(ss.at[:, sent], sr.at[:, sent], s_s, s_r.at[0], (me, z)).wait_send()
    last_block, last_cols = piece(last)

    def finish_half(h):
        rows = part_rows(h, half)
        rest = dot(wd[rows, weight_cols(last)], sr[last_block, :, last_cols], NT)
        back = backs[rows] + rest
        dgu[pl.ds(pl.multiple_of(2 * h * half, 2 * half), half)] = (
            back * slope[rows]
        ).astype(BF16)
        dgu[pl.ds(pl.multiple_of((2 * h + 1) * half, half), half)] = (
            back * silus[rows]
        ).astype(BF16)
        return jnp.sum(act[rows].astype(F32) * back, axis=0, keepdims=True)

    def gate_up_half(h, c):
        return dot(dgu[part_rows(h, 2 * half)], xr[c], NN)

    def gate_up_copy(k, c):
        dst = (far_gu.at[0], far_gu.at[1], mid_gu.at[1], mid_gu.at[0], near_gu.at[0], near_gu.at[1])
        size = 2 * half
        if k < 5:
            src = ss.at[c, k * size : (k + 1) * size]
        else:
            src = xs.at[c, 6 * half : 6 * half + size]
        return src, remote(
            src,
            dst[k].at[c],
            gu_s.at[k, c],
            gu_r.at[k, c],
            (me, up if k % 2 == 0 else down),
        )

    def send_gate_up(k, c):
        value = gate_up_half(halves[k], c)
        src, copy = gate_up_copy(k, c)
        if k >= 4:
            gate_up_copy(k - 4, c)[1].wait_recv()
            value = value + far_gu[k - 4, c].astype(F32)
        src[...] = value.astype(BF16)
        copy.start()

    def return_tile(g, n):
        at = slice(g * ROWS, (g + 1) * ROWS)
        cols = pl.ds(pl.multiple_of(n * COLS, COLS), COLS)
        back_s[n, at] = dot(dgu[:, at], wgu[:, cols], TN).astype(BF16)
        for i in range(max(1, g * GROUP), (g + 1) * GROUP):
            rows = slice(i * CAP, (i + 1) * CAP)
            remote(
                back_s.at[n, rows],
                back_r.at[n, rows],
                back_ss,
                back_rs.at[n],
                (source(i), z),
            ).start()

    total = finish_half(halves[0]) + finish_half(halves[1])
    send_gate_up(0, 0)
    send_gate_up(1, 0)
    total = lax.fori_loop(
        2, HALVES, lambda i, t: t + finish_half((2 * across + i) % HALVES), total
    )

    def with_far(n, _):
        return_tile(0, n)

        @pl.when(n < chunks - 1)
        def _():
            send_gate_up(0, n + 1)
            send_gate_up(1, n + 1)

        return 0

    lax.fori_loop(0, chunks, with_far, 0)

    def with_near(n, _):
        return_tile(1, n)
        send_gate_up(2, n)
        send_gate_up(3, n)
        return 0

    lax.fori_loop(0, chunks, with_near, 0)

    high = total.astype(BF16).astype(F32)
    line = lax.broadcasted_iota(jnp.int32, (128, n_shift * CAP), 0)
    pair = jnp.where(line == 0, high, jnp.where(line == 1, total - high, 0.0))
    prob_s[...] = pair.T.astype(BF16)
    for i in range(1, n_shift):
        rows = slice(i * CAP, (i + 1) * CAP)
        remote(
            prob_s.at[rows], prob_r.at[rows], prob_ss, prob_rs, (source(i), z)
        ).start()
    down_first(last)

    def rest_back(n, _):
        return_tile(2, n)
        return_tile(3, n)
        return 0

    lax.fori_loop(0, chunks, rest_back, 0)

    def with_far_sum(c, _):
        send_gate_up(4, c)
        send_gate_up(5, c)
        return 0

    lax.fori_loop(0, chunks, with_far_sum, 0)
    down_second(last)
    for part in range(2):

        def keep(c, _, part=part):
            value = gate_up_half(2 * z + part, c)
            gate_up_copy(3 - part, c)[1].wait_recv()
            value = value + mid_gu[part, c].astype(F32)
            rows = part_rows(part * chunks + c, half)
            slope[rows, 0:COLS] = value[0:half]
            slope[rows, COLS : 2 * COLS] = value[half : 2 * half]
            return 0

        lax.fori_loop(0, chunks, keep, 0)
        for j in range(last + 1):
            down_copy(3 - part, j).wait_recv()
        for c in range(chunks):
            at = slice((part * chunks + c) * half, (part * chunks + c + 1) * half)
            own_d[at] = own_d[at] + mid_d[part, c].astype(F32)
    back_r[:, 0:CAP] = back_s[:, 0:CAP]
    prob_r[0:CAP] = prob_s[0:CAP]
    remote(prob_s.at[sent], prob_r.at[sent], prob_ss, prob_rs, (me, z)).wait_recv()
    for k in range(2):
        terms = dot(pick[k], prob_r[...], NN).T
        dprob_ref[k : k + 1] = (
            jnp.sum(terms, axis=0, keepdims=True) / probs_ref[...].astype(F32)[k : k + 1]
        )

    def token_copy(n):
        cols = pl.ds(pl.multiple_of(n * COLS, COLS), COLS)
        return pltpu.make_async_copy(dtok_ref.at[n], dtok_hbm.at[:, cols], dtok_sem.at[n])

    def combine(n, _):
        remote(
            back_s.at[n, sent], back_r.at[n, sent], back_ss, back_rs.at[n], (me, z)
        ).wait_recv()
        both = pick[0] + pick[1]
        dtok_ref[n] = dot(both, back_r[n], NN).astype(BF16)
        token_copy(n).start()
        return 0

    def sum_copy(j, part, c):
        src, dst = ((near_gu, sum_gu_hbm), (near_d, sum_d_hbm))[j]
        return pltpu.make_async_copy(
            src.at[part, c], dst.at[part, c], sum_sem.at[j, part, c]
        )

    def complete(c, _):
        for part in range(2):
            gate_up_copy(4 + part, c)[1].wait_recv()
            rows = part_rows(part * chunks + c, half)
            for j in range(2):
                at = slice(j * half, (j + 1) * half)
                value = slope[rows, j * COLS : (j + 1) * COLS]
                near_gu[part, c, at] = (value + near_gu[part, c, at].astype(F32)).astype(BF16)
            sum_copy(0, part, c).start()
        return 0

    def combine_and_complete(c, _):
        combine(c, 0)
        return complete(c, 0)

    lax.fori_loop(0, chunks, combine_and_complete, 0)

    for j in range(last + 1):
        for part in range(2):
            down_copy(4 + part, j).wait_recv()

    def complete_down(c, _):
        for part in range(2):
            value = own_d[part_rows(part * chunks + c, half)]
            near_d[part, c] = (value + near_d[part, c].astype(F32)).astype(BF16)
            sum_copy(1, part, c).start()
        return 0

    lax.fori_loop(0, chunks, complete_down, 0)
    for k in range(6):
        for j in range(last + 1):
            down_copy(k, j).wait_send()

    def finish(c, _):
        token_copy(c).wait()
        for k in range(6):
            gate_up_copy(k, c)[1].wait_send()
        for part in range(2):
            for j in range(2):
                sum_copy(j, part, c).wait()
        return 0

    lax.fori_loop(0, chunks, finish, 0)
    remote(
        back_s.at[:, sent], back_r.at[:, sent], back_ss, back_rs.at[0], (me, z)
    ).wait_send()
    remote(prob_s.at[sent], prob_r.at[sent], prob_ss, prob_rs, (me, z)).wait_send()


def widen(
    sum_gu_hbm,
    sum_d_hbm,
    tok_in,
    prob_in,
    tok_out,
    prob_out,
    gg_hbm,
    gu_hbm,
    gd_hbm,
    sum_gu,
    sum_d,
    tok,
    wide,
    in_sem,
    out_sem,
    tok_sem,
):
    parts, chunks, half = sum_d.shape[0:3]
    tiles = [(p, c) for c in range(chunks) for p in range(parts)]
    loads = {}
    for t in tiles:
        loads[t] = [
            pltpu.make_async_copy(sum_gu_hbm.at[t], sum_gu.at[t], in_sem.at[t + (0,)]),
            pltpu.make_async_copy(sum_d_hbm.at[t], sum_d.at[t], in_sem.at[t + (1,)]),
        ]
        for load in loads[t]:
            load.start()
    tok_load = pltpu.make_async_copy(tok_in, tok, tok_sem.at[0])
    tok_load.start()
    prob_out[...] = prob_in[...]
    stores = []
    for p, c in tiles:
        for load in loads[p, c]:
            load.wait()
        wide[p, c, 0] = sum_gu[p, c, 0:half].astype(F32)
        wide[p, c, 1] = sum_gu[p, c, half : 2 * half].astype(F32)
        wide[p, c, 2] = sum_d[p, c].astype(F32)
        low = slice(p * half, (p + 1) * half)
        cols = slice(c * COLS, (c + 1) * COLS)
        for j, out in enumerate((gg_hbm, gu_hbm, gd_hbm)):
            store = pltpu.make_async_copy(
                wide.at[p, c, j], out.at[low, cols], out_sem.at[p, c, j]
            )
            store.start()
            stores.append(store)
    tok_load.wait()
    stores.append(pltpu.make_async_copy(tok, tok_out, tok_sem.at[1]))
    stores[-1].start()
    for store in stores:
        store.wait()


def per_device(tokens, grad_out, routes, gate_probs, w_gate, w_up, w_down):
    n_tok, width = tokens.shape
    hidden = w_gate.shape[1]
    half = hidden // HALVES
    slots = len(SHIFTS) * CAP
    chunks = width // COLS
    vmem = pl.BlockSpec(memory_space=pltpu.VMEM)
    hbm = pl.BlockSpec(memory_space=pl.ANY)
    weights = [w[0] for w in (w_gate, w_up, w_down)]
    dma = pltpu.SemaphoreType.DMA
    d_tokens, d_probs, sum_gu, sum_d = pl.pallas_call(
        kernel,
        out_shape=(
            jax.ShapeDtypeStruct((n_tok, width), BF16),
            jax.ShapeDtypeStruct((2, n_tok), F32),
            jax.ShapeDtypeStruct((2, chunks, 2 * half, COLS), BF16),
            jax.ShapeDtypeStruct((2, chunks, half, COLS), BF16),
        ),
        in_specs=[vmem, hbm, vmem, vmem] + [hbm] * 3,
        out_specs=[hbm, vmem, hbm, hbm],
        scratch_shapes=[
            pltpu.VMEM((n_tok, width), BF16),
            pltpu.VMEM((chunks, n_tok, COLS), BF16),
            pltpu.VMEM((2, n_tok, slots), BF16),
            pltpu.VMEM((n_tok, slots), BF16),
            pltpu.VMEM((chunks, slots, COLS), BF16),
            pltpu.VMEM((chunks, slots, COLS), BF16),
            pltpu.VMEM((chunks, slots, COLS), BF16),
            pltpu.VMEM((chunks, slots, COLS), BF16),
            pltpu.VMEM((2 * hidden, width), BF16),
            pltpu.VMEM((hidden, width), BF16),
            pltpu.VMEM((2 * hidden, slots), BF16),
            pltpu.VMEM((hidden, slots), BF16),
            pltpu.VMEM((hidden, slots), F32),
            pltpu.VMEM((hidden, slots), F32),
            pltpu.VMEM((hidden, slots), F32),
            pltpu.VMEM((hidden, COLS), F32),
            pltpu.VMEM((chunks, slots, COLS), BF16),
            pltpu.VMEM((chunks, slots, COLS), BF16),
            pltpu.VMEM((slots, 128), BF16),
            pltpu.VMEM((slots, 128), BF16),
            pltpu.VMEM((2, chunks, 2 * half, COLS), BF16),
            pltpu.VMEM((2, chunks, half, COLS), BF16),
            pltpu.VMEM((2, chunks, 2 * half, COLS), BF16),
            pltpu.VMEM((2, chunks, half, COLS), BF16),
            pltpu.VMEM((2, chunks, 2 * half, COLS), BF16),
            pltpu.VMEM((2, chunks, half, COLS), BF16),
            dma((1 + 2 * HALVES,)),
            dma,
            dma((len(SHIFTS) // GROUP,)),
            dma,
            dma((len(PIECES),)),
            dma,
            dma((chunks,)),
            dma,
            dma,
            dma((6, chunks)),
            dma((6, chunks)),
            dma((6, len(PIECES))),
            dma((6, len(PIECES))),
            dma((2, 2, chunks)),
            dma,
            dma((chunks,)),
        ],
        compiler_params=pltpu.CompilerParams(
            collective_id=0, has_side_effects=True, vmem_limit_bytes=63 << 20
        ),
        name="routed_backward",
    )(tokens, grad_out, routes.T, gate_probs.T, *weights)
    shard = jax.ShapeDtypeStruct((hidden // 4, width), F32)
    d_tokens, d_probs, grad_g, grad_u, grad_d = pl.pallas_call(
        widen,
        out_shape=(
            jax.ShapeDtypeStruct((n_tok, width), BF16),
            jax.ShapeDtypeStruct((2, n_tok), F32),
            shard,
            shard,
            shard,
        ),
        in_specs=[hbm] * 3 + [vmem],
        out_specs=[hbm, vmem] + [hbm] * 3,
        scratch_shapes=[
            pltpu.VMEM((2, chunks, 2 * half, COLS), BF16),
            pltpu.VMEM((2, chunks, half, COLS), BF16),
            pltpu.VMEM((n_tok, width), BF16),
            pltpu.VMEM((2, chunks, 3, half, COLS), F32),
            dma((2, chunks, 2)),
            dma((2, chunks, 3)),
            dma((2,)),
        ],
        compiler_params=pltpu.CompilerParams(vmem_limit_bytes=62 << 20),
        name="widen",
    )(sum_gu, sum_d, d_tokens, d_probs)
    return d_tokens, d_probs.T, grad_g[None], grad_u[None], grad_d[None]


def solution(mesh):
    rows, experts = P(("expert", "dp"), None), P("expert", None, None)
    split = P("expert", "dp", None)
    return jax.shard_map(
        per_device,
        mesh=mesh,
        in_specs=(rows, rows, rows, rows, experts, experts, experts),
        out_specs=(rows, rows, split, split, split),
        check_vma=False,
    )
```

```python
import functools

import jax
import jax.numpy as jnp
from jax import lax
from jax.experimental import pallas as pl
from jax.experimental.pallas import tpu as pltpu
from jax.sharding import PartitionSpec as P

F32 = jnp.float32
BF16 = jnp.bfloat16
MESH = pl.DeviceIdType.MESH
NT = (((1,), (1,)), ((), ()))
TN = (((0,), (0,)), ((), ()))
NN = (((1,), (0,)), ((), ()))

RINGS = (
    ((2, 0), (0, 2), (2, 2)),
    ((2, 1), (1, 2), (2, 3), (3, 2)),
    ((1, 1), (3, 3), (1, 3), (3, 1)),
    ((1, 0), (0, 1), (3, 0), (0, 3)),
)
SHIFTS = [(0, 0, 0), (0, 0, 1)] + [
    (dx, dy, dc) for ring in RINGS for dc in (0, 1) for dx, dy in ring
]
CAP = 32
PROB_ROWS = CAP // 2
GROUP = 8
ROWS = GROUP * CAP
COLS = 512
PIECES = ((0, 0, 512), (1, 0, 512), (2, 0, 512), (3, 0, 256), (3, 256, 256))
HALVES = 8


def dot(a, b, dims):
    return lax.dot_general(a, b, dims, preferred_element_type=F32)


def kernel(
    tok_hbm,
    dy_hbm,
    routes_ref,
    probs_ref,
    wg_hbm,
    wu_hbm,
    wd_hbm,
    dtok_hbm,
    dprob_ref,
    sum_gu_hbm,
    sum_d_hbm,
    tok_ref,
    dy_ref,
    dtok_ref,
    pick,
    pick_scaled,
    xs,
    ss,
    xr,
    sr,
    wgu,
    wd,
    dgu,
    act,
    slope,
    silus,
    backs,
    own_d,
    back_s,
    back_r,
    prob_s,
    prob_r,
    far_gu,
    far_d,
    mid_gu,
    mid_d,
    near_gu,
    near_d,
    w_sem,
    x_s,
    x_r,
    s_s,
    s_r,
    back_ss,
    back_rs,
    prob_ss,
    prob_rs,
    gu_s,
    gu_r,
    d_s,
    d_r,
    sum_sem,
    tok_sem,
    dy_sem,
    dtok_sem,
):
    me, z = lax.axis_index("expert"), lax.axis_index("dp")
    cx, cy, core = me // 8, (me // 2) % 4, me % 2
    up, down, across = (z + 1) % 4, (z + 3) % 4, (z + 2) % 4
    n_shift = len(SHIFTS)
    groups = n_shift // GROUP
    n_tok, width = tok_ref.shape
    chunks = width // COLS
    half = wd.shape[0] // HALVES

    def owner(i):
        dx, dy, dc = SHIFTS[i]
        return ((cx + dx) % 4) * 8 + ((cy + dy) % 4) * 2 + (core + dc) % 2

    def source(i):
        dx, dy, dc = SHIFTS[i]
        return ((cx + 4 - dx) % 4) * 8 + ((cy + 4 - dy) % 4) * 2 + (core + dc) % 2

    def remote(src, dst, send_sem, recv_sem, device):
        return pltpu.make_async_remote_copy(
            src_ref=src,
            dst_ref=dst,
            send_sem=send_sem,
            recv_sem=recv_sem,
            device_id=device,
            device_id_type=MESH,
        )

    barrier = pltpu.get_barrier_semaphore()
    for i in range(1, n_shift):
        pl.semaphore_signal(barrier, inc=1, device_id=(owner(i), z), device_id_type=MESH)
    for other in (up, down):
        pl.semaphore_signal(barrier, inc=1, device_id=(me, other), device_id_type=MESH)

    tok_load = pltpu.make_async_copy(tok_hbm, tok_ref, tok_sem)
    tok_load.start()
    dy_load = pltpu.make_async_copy(dy_hbm, dy_ref, dy_sem)
    loads = [
        pltpu.make_async_copy(wd_hbm, wd, w_sem.at[0]),
    ]
    for h in range(HALVES):
        for j, w in enumerate((wg_hbm, wu_hbm)):
            loads.append(
                pltpu.make_async_copy(
                    w.at[h * half : (h + 1) * half],
                    wgu.at[(2 * h + j) * half : (2 * h + j + 1) * half],
                    w_sem.at[1 + 2 * h + j],
                )
            )

    line = lax.broadcasted_iota(jnp.int32, (128, n_tok), 0)
    routes = routes_ref[...].astype(F32)
    probs = probs_ref[...].astype(F32)
    table = jnp.where(line == 0, routes[0:1], routes[1:2])
    table = jnp.where(line == 2, probs[0:1], table)
    table = jnp.where(line == 3, probs[1:2], table).T
    lane = lax.broadcasted_iota(jnp.int32, (n_tok, 128), 1)
    place = jnp.zeros((1, 128), jnp.int32)
    for i in range(1, n_shift):
        place = place + jnp.where(lane[0:1] == owner(i), i * CAP, 0)
    earlier = (
        lax.broadcasted_iota(jnp.int32, (n_tok, n_tok), 0)
        > lax.broadcasted_iota(jnp.int32, (n_tok, n_tok), 1)
    )
    earlier = jnp.where(earlier, 1.0, 0.0).astype(BF16)
    slot = lax.broadcasted_iota(jnp.int32, (n_tok, ROWS), 1)
    offset = place.astype(F32)
    targets = []
    for k in range(2):
        named = lane == table[:, k : k + 1].astype(jnp.int32)
        hot = jnp.where(named, 1.0, 0.0)
        rank = dot(earlier, hot.astype(BF16), NN) + offset
        offset = offset + jnp.sum(hot, axis=0, keepdims=True)
        target = jnp.sum(jnp.where(named, rank, 0.0), axis=1, keepdims=True)
        targets.append(target.astype(jnp.int32))

    tok_load.wait()
    for g in range(groups):
        at = slice(g * ROWS, (g + 1) * ROWS)
        chosen = [slot == target - g * ROWS for target in targets]
        both = jnp.where(chosen[0] | chosen[1], 1.0, 0.0).astype(BF16)
        for c in range(chunks):
            cols = slice(c * COLS, (c + 1) * COLS)
            xs[c, at] = dot(both, tok_ref[:, cols], TN).astype(BF16)
            if g == 0 and c == 0:
                pl.semaphore_wait(barrier, n_shift + 1)
            for i in range(max(1, g * GROUP), (g + 1) * GROUP):
                rows = slice(i * CAP, (i + 1) * CAP)
                remote(
                    xs.at[c, rows], xr.at[c, rows], x_s, x_r.at[g], (owner(i), z)
                ).start()
        if g == 0:
            for load in [dy_load] + loads:
                load.start()
        scaled = jnp.zeros((n_tok, ROWS), F32)
        for k in range(2):
            pick[k, :, at] = jnp.where(chosen[k], 1.0, 0.0).astype(BF16)
            scaled = scaled + jnp.where(chosen[k], table[:, 2 + k : 3 + k], 0.0)
        pick_scaled[:, at] = scaled.astype(BF16)
    dy_load.wait()
    for c in range(chunks):
        cols = slice(c * COLS, (c + 1) * COLS)
        for g in range(groups):
            at = slice(g * ROWS, (g + 1) * ROWS)
            ss[c, at] = dot(pick_scaled[:, at], dy_ref[:, cols], TN).astype(BF16)
        for j, (block, low, size) in enumerate(PIECES):
            for i in range(1, n_shift) if block == c else ():
                at = (c, slice(i * CAP, (i + 1) * CAP), slice(low, low + size))
                remote(ss.at[at], sr.at[at], s_s, s_r.at[j], (owner(i), z)).start()
    for c in range(chunks):
        xr[c, 0:CAP] = xs[c, 0:CAP]
        sr[c, 0:CAP] = ss[c, 0:CAP]
    for load in loads:
        load.wait()

    for g in range(groups):
        first = CAP if g == 0 else g * ROWS
        took = slice(first, (g + 1) * ROWS)
        remote(xs.at[:, took], xr.at[:, took], x_s, x_r.at[g], (me, z)).wait_recv()
        at = slice(g * ROWS, (g + 1) * ROWS)

        def project(t, _, at=at):
            rows = pl.ds(pl.multiple_of(t * 4 * half, 4 * half), 4 * half)
            pre = jnp.zeros((4 * half, ROWS), F32)
            for c in range(chunks):
                cols = slice(c * COLS, (c + 1) * COLS)
                pre = pre + dot(wgu[rows, cols], xr[c, at], NT)
            for j in range(2):
                gate = pre[2 * j * half : (2 * j + 1) * half]
                upward = pre[(2 * j + 1) * half : (2 * j + 2) * half]
                into = pl.ds(pl.multiple_of((2 * t + j) * half, half), half)
                sig = jax.nn.sigmoid(gate)
                silu = gate * sig
                act[into, at] = (silu * upward).astype(BF16)
                slope[into, at] = upward * (sig + silu * (1.0 - sig))
                silus[into, at] = silu
            return 0

        lax.fori_loop(0, HALVES // 2, project, 0)

    sent = slice(CAP, n_shift * CAP)
    remote(xs.at[:, sent], xr.at[:, sent], x_s, x_r.at[0], (me, z)).wait_send()

    def part_rows(h, size):
        return pl.ds(pl.multiple_of(h * size, size), size)

    def piece(j):
        block, low, size = PIECES[j]
        return block, slice(low, low + size)

    def down_half(h, j):
        block, cols = piece(j)
        return dot(act[part_rows(h, half)], sr[block, :, cols], NN)

    D_ROWS = [slice(k * half, (k + 1) * half) for k in range(6)]

    def down_copy(k, j):
        block, cols = piece(j)
        dst = (far_d.at[0], far_d.at[1], mid_d.at[1], mid_d.at[0], near_d.at[0], near_d.at[1])
        return remote(
            xs.at[block, D_ROWS[k], cols],
            dst[k].at[block, :, cols],
            d_s.at[k, j],
            d_r.at[k, j],
            (me, up if k % 2 == 0 else down),
        )

    halves = (2 * across, 2 * across + 1, 2 * up + 1, 2 * down, 2 * up, 2 * down + 1)

    def down_first(j):
        block, cols = piece(j)
        for k in range(4):
            xs[block, D_ROWS[k], cols] = down_half(halves[k], j).astype(BF16)
            down_copy(k, j).start()
        for part in range(2):
            at = (part * chunks + block) * half
            own_d[at : at + half, cols] = down_half(2 * z + part, j)

    def down_second(j):
        block, cols = piece(j)
        for k in range(4, 6):
            value = down_half(halves[k], j)
            down_copy(k - 4, j).wait_recv()
            value = value + far_d[k - 4, block, :, cols].astype(F32)
            xs[block, D_ROWS[k], cols] = value.astype(BF16)
            down_copy(k, j).start()

    def piece_arrived(j):
        block, cols = piece(j)
        at = (block, sent, cols)
        remote(ss.at[at], sr.at[at], s_s, s_r.at[j], (me, z)).wait_recv()

    def weight_cols(j):
        block, low, size = PIECES[j]
        return slice(block * COLS + low, block * COLS + low + size)

    big = 4 * half
    last = len(PIECES) - 1
    for j in range(last):
        block, cols = piece(j)
        piece_arrived(j)
        down_first(j)

        def project_back(t, _, j=j, block=block, cols=cols):
            rows = part_rows(t, big)
            value = dot(wd[rows, weight_cols(j)], sr[block, :, cols], NT)
            backs[rows] = value if j == 0 else backs[rows] + value
            return 0

        lax.fori_loop(0, HALVES // 4, project_back, 0)
        down_second(j)

    piece_arrived(last)
    remote(ss.at[:, sent], sr.at[:, sent], s_s, s_r.at[0], (me, z)).wait_send()
    last_block, last_cols = piece(last)

    def finish_half(h):
        rows = part_rows(h, half)
        rest = dot(wd[rows, weight_cols(last)], sr[last_block, :, last_cols], NT)
        back = backs[rows] + rest
        dgu[pl.ds(pl.multiple_of(2 * h * half, 2 * half), half)] = (
            back * slope[rows]
        ).astype(BF16)
        dgu[pl.ds(pl.multiple_of((2 * h + 1) * half, half), half)] = (
            back * silus[rows]
        ).astype(BF16)
        return jnp.sum(act[rows].astype(F32) * back, axis=0, keepdims=True)

    def gate_up_half(h, c):
        return dot(dgu[part_rows(h, 2 * half)], xr[c], NN)

    def gate_up_copy(k, c):
        dst = (far_gu.at[0], far_gu.at[1], mid_gu.at[1], mid_gu.at[0], near_gu.at[0], near_gu.at[1])
        size = 2 * half
        if k < 5:
            src = ss.at[c, k * size : (k + 1) * size]
        else:
            src = xs.at[c, 6 * half : 6 * half + size]
        return src, remote(
            src,
            dst[k].at[c],
            gu_s.at[k, c],
            gu_r.at[k, c],
            (me, up if k % 2 == 0 else down),
        )

    def send_gate_up(k, c):
        value = gate_up_half(halves[k], c)
        src, copy = gate_up_copy(k, c)
        if k >= 4:
            gate_up_copy(k - 4, c)[1].wait_recv()
            value = value + far_gu[k - 4, c].astype(F32)
        src[...] = value.astype(BF16)
        copy.start()

    def return_tile(g, n):
        at = slice(g * ROWS, (g + 1) * ROWS)
        cols = pl.ds(pl.multiple_of(n * COLS, COLS), COLS)
        back_s[n, at] = dot(dgu[:, at], wgu[:, cols], TN).astype(BF16)
        for i in range(max(1, g * GROUP), (g + 1) * GROUP):
            rows = slice(i * CAP, (i + 1) * CAP)
            remote(
                back_s.at[n, rows],
                back_r.at[n, rows],
                back_ss,
                back_rs.at[n],
                (source(i), z),
            ).start()

    total = finish_half(halves[0]) + finish_half(halves[1])
    send_gate_up(0, 0)
    send_gate_up(1, 0)
    total = lax.fori_loop(
        2, HALVES, lambda i, t: t + finish_half((2 * across + i) % HALVES), total
    )

    def with_far(n, _):
        return_tile(0, n)

        @pl.when(n < chunks - 1)
        def _():
            send_gate_up(0, n + 1)
            send_gate_up(1, n + 1)

        return 0

    lax.fori_loop(0, chunks, with_far, 0)

    def with_near(n, _):
        return_tile(1, n)
        send_gate_up(2, n)
        send_gate_up(3, n)
        return 0

    lax.fori_loop(0, chunks, with_near, 0)

    high = total.astype(BF16).astype(F32)
    line = lax.broadcasted_iota(jnp.int32, (128, n_shift * CAP), 0)
    upper = lax.broadcasted_iota(jnp.int32, (128, n_shift * CAP), 1) % CAP // PROB_ROWS
    pair = jnp.where(line == 2 * upper, high, 0.0)
    pair = jnp.where(line == 2 * upper + 1, total - high, pair)
    pair = pair.T.reshape(n_shift, 2, PROB_ROWS, 128)
    pair = (pair[:, 0] + pair[:, 1]).astype(BF16)
    prob_s[...] = pair.reshape(n_shift * PROB_ROWS, 128)
    prob_sent = slice(PROB_ROWS, n_shift * PROB_ROWS)
    for i in range(1, n_shift):
        rows = slice(i * PROB_ROWS, (i + 1) * PROB_ROWS)
        remote(
            prob_s.at[rows], prob_r.at[rows], prob_ss, prob_rs, (source(i), z)
        ).start()
    down_first(last)

    def rest_back(n, _):
        return_tile(2, n)
        return_tile(3, n)
        return 0

    lax.fori_loop(0, chunks, rest_back, 0)

    def with_far_sum(c, _):
        send_gate_up(4, c)
        send_gate_up(5, c)
        return 0

    lax.fori_loop(0, chunks, with_far_sum, 0)
    down_second(last)
    for part in range(2):

        def keep(c, _, part=part):
            value = gate_up_half(2 * z + part, c)
            gate_up_copy(3 - part, c)[1].wait_recv()
            value = value + mid_gu[part, c].astype(F32)
            rows = part_rows(part * chunks + c, half)
            slope[rows, 0:COLS] = value[0:half]
            slope[rows, COLS : 2 * COLS] = value[half : 2 * half]
            return 0

        lax.fori_loop(0, chunks, keep, 0)
        for j in range(last + 1):
            down_copy(3 - part, j).wait_recv()
        for c in range(chunks):
            at = slice((part * chunks + c) * half, (part * chunks + c + 1) * half)
            own_d[at] = own_d[at] + mid_d[part, c].astype(F32)
    back_r[:, 0:CAP] = back_s[:, 0:CAP]
    prob_r[0:PROB_ROWS] = prob_s[0:PROB_ROWS]
    remote(
        prob_s.at[prob_sent], prob_r.at[prob_sent], prob_ss, prob_rs, (me, z)
    ).wait_recv()
    terms = prob_r[...].astype(F32).reshape(n_shift, PROB_ROWS, 128)
    column = lax.broadcasted_iota(jnp.int32, terms.shape, 2)
    terms = jnp.stack(
        [jnp.where(column < 2, terms, 0.0), jnp.where(column >= 2, terms, 0.0)], axis=1
    )
    terms = terms.reshape(n_shift * CAP, 128).astype(BF16)
    for k in range(2):
        mine = dot(pick[k], terms, NN).T
        dprob_ref[k : k + 1] = (
            jnp.sum(mine, axis=0, keepdims=True) / probs_ref[...].astype(F32)[k : k + 1]
        )

    def token_copy(n):
        cols = pl.ds(pl.multiple_of(n * COLS, COLS), COLS)
        return pltpu.make_async_copy(dtok_ref.at[n], dtok_hbm.at[:, cols], dtok_sem.at[n])

    def combine(n, _):
        remote(
            back_s.at[n, sent], back_r.at[n, sent], back_ss, back_rs.at[n], (me, z)
        ).wait_recv()
        both = pick[0] + pick[1]
        dtok_ref[n] = dot(both, back_r[n], NN).astype(BF16)
        token_copy(n).start()
        return 0

    def sum_copy(j, part, c):
        src, dst = ((near_gu, sum_gu_hbm), (near_d, sum_d_hbm))[j]
        return pltpu.make_async_copy(
            src.at[part, c], dst.at[part, c], sum_sem.at[j, part, c]
        )

    def complete(c, _):
        for part in range(2):
            gate_up_copy(4 + part, c)[1].wait_recv()
            rows = part_rows(part * chunks + c, half)
            for j in range(2):
                at = slice(j * half, (j + 1) * half)
                value = slope[rows, j * COLS : (j + 1) * COLS]
                near_gu[part, c, at] = (value + near_gu[part, c, at].astype(F32)).astype(BF16)
            sum_copy(0, part, c).start()
        return 0

    def combine_and_complete(c, _):
        combine(c, 0)
        return complete(c, 0)

    lax.fori_loop(0, chunks, combine_and_complete, 0)

    for j in range(last + 1):
        for part in range(2):
            down_copy(4 + part, j).wait_recv()

    def complete_down(c, _):
        for part in range(2):
            value = own_d[part_rows(part * chunks + c, half)]
            near_d[part, c] = (value + near_d[part, c].astype(F32)).astype(BF16)
            sum_copy(1, part, c).start()
        return 0

    lax.fori_loop(0, chunks, complete_down, 0)
    for k in range(6):
        for j in range(last + 1):
            down_copy(k, j).wait_send()

    def finish(c, _):
        token_copy(c).wait()
        for k in range(6):
            gate_up_copy(k, c)[1].wait_send()
        for part in range(2):
            for j in range(2):
                sum_copy(j, part, c).wait()
        return 0

    lax.fori_loop(0, chunks, finish, 0)
    remote(
        back_s.at[:, sent], back_r.at[:, sent], back_ss, back_rs.at[0], (me, z)
    ).wait_send()
    remote(
        prob_s.at[prob_sent], prob_r.at[prob_sent], prob_ss, prob_rs, (me, z)
    ).wait_send()


def widen(
    sum_gu_hbm,
    sum_d_hbm,
    tok_in,
    prob_in,
    tok_out,
    prob_out,
    gg_hbm,
    gu_hbm,
    gd_hbm,
    sum_gu,
    sum_d,
    tok,
    wide,
    in_sem,
    out_sem,
    tok_sem,
):
    parts, chunks, half = sum_d.shape[0:3]
    tiles = [(p, c) for c in range(chunks) for p in range(parts)]
    loads = {}
    for t in tiles:
        loads[t] = [
            pltpu.make_async_copy(sum_gu_hbm.at[t], sum_gu.at[t], in_sem.at[t + (0,)]),
            pltpu.make_async_copy(sum_d_hbm.at[t], sum_d.at[t], in_sem.at[t + (1,)]),
        ]
        for load in loads[t]:
            load.start()
    tok_load = pltpu.make_async_copy(tok_in, tok, tok_sem.at[0])
    tok_load.start()
    prob_out[...] = prob_in[...]
    stores = []
    for p, c in tiles:
        for load in loads[p, c]:
            load.wait()
        wide[p, c, 0] = sum_gu[p, c, 0:half].astype(F32)
        wide[p, c, 1] = sum_gu[p, c, half : 2 * half].astype(F32)
        wide[p, c, 2] = sum_d[p, c].astype(F32)
        low = slice(p * half, (p + 1) * half)
        cols = slice(c * COLS, (c + 1) * COLS)
        for j, out in enumerate((gg_hbm, gu_hbm, gd_hbm)):
            store = pltpu.make_async_copy(
                wide.at[p, c, j], out.at[low, cols], out_sem.at[p, c, j]
            )
            store.start()
            stores.append(store)
    tok_load.wait()
    stores.append(pltpu.make_async_copy(tok, tok_out, tok_sem.at[1]))
    stores[-1].start()
    for store in stores:
        store.wait()


def per_device(tokens, grad_out, routes, gate_probs, w_gate, w_up, w_down):
    n_tok, width = tokens.shape
    hidden = w_gate.shape[1]
    half = hidden // HALVES
    slots = len(SHIFTS) * CAP
    chunks = width // COLS
    vmem = pl.BlockSpec(memory_space=pltpu.VMEM)
    hbm = pl.BlockSpec(memory_space=pl.ANY)
    weights = [w[0] for w in (w_gate, w_up, w_down)]
    dma = pltpu.SemaphoreType.DMA
    d_tokens, d_probs, sum_gu, sum_d = pl.pallas_call(
        kernel,
        out_shape=(
            jax.ShapeDtypeStruct((n_tok, width), BF16),
            jax.ShapeDtypeStruct((2, n_tok), F32),
            jax.ShapeDtypeStruct((2, chunks, 2 * half, COLS), BF16),
            jax.ShapeDtypeStruct((2, chunks, half, COLS), BF16),
        ),
        in_specs=[hbm, hbm, vmem, vmem] + [hbm] * 3,
        out_specs=[hbm, vmem, hbm, hbm],
        scratch_shapes=[
            pltpu.VMEM((n_tok, width), BF16),
            pltpu.VMEM((n_tok, width), BF16),
            pltpu.VMEM((chunks, n_tok, COLS), BF16),
            pltpu.VMEM((2, n_tok, slots), BF16),
            pltpu.VMEM((n_tok, slots), BF16),
            pltpu.VMEM((chunks, slots, COLS), BF16),
            pltpu.VMEM((chunks, slots, COLS), BF16),
            pltpu.VMEM((chunks, slots, COLS), BF16),
            pltpu.VMEM((chunks, slots, COLS), BF16),
            pltpu.VMEM((2 * hidden, width), BF16),
            pltpu.VMEM((hidden, width), BF16),
            pltpu.VMEM((2 * hidden, slots), BF16),
            pltpu.VMEM((hidden, slots), BF16),
            pltpu.VMEM((hidden, slots), F32),
            pltpu.VMEM((hidden, slots), F32),
            pltpu.VMEM((hidden, slots), F32),
            pltpu.VMEM((hidden, COLS), F32),
            pltpu.VMEM((chunks, slots, COLS), BF16),
            pltpu.VMEM((chunks, slots, COLS), BF16),
            pltpu.VMEM((slots // 2, 128), BF16),
            pltpu.VMEM((slots // 2, 128), BF16),
            pltpu.VMEM((2, chunks, 2 * half, COLS), BF16),
            pltpu.VMEM((2, chunks, half, COLS), BF16),
            pltpu.VMEM((2, chunks, 2 * half, COLS), BF16),
            pltpu.VMEM((2, chunks, half, COLS), BF16),
            pltpu.VMEM((2, chunks, 2 * half, COLS), BF16),
            pltpu.VMEM((2, chunks, half, COLS), BF16),
            dma((1 + 2 * HALVES,)),
            dma,
            dma((len(SHIFTS) // GROUP,)),
            dma,
            dma((len(PIECES),)),
            dma,
            dma((chunks,)),
            dma,
            dma,
            dma((6, chunks)),
            dma((6, chunks)),
            dma((6, len(PIECES))),
            dma((6, len(PIECES))),
            dma((2, 2, chunks)),
            dma,
            dma,
            dma((chunks,)),
        ],
        compiler_params=pltpu.CompilerParams(
            collective_id=0, has_side_effects=True, vmem_limit_bytes=63 << 20
        ),
        name="routed_backward",
    )(tokens, grad_out, routes.T, gate_probs.T, *weights)
    shard = jax.ShapeDtypeStruct((hidden // 4, width), F32)
    d_tokens, d_probs, grad_g, grad_u, grad_d = pl.pallas_call(
        widen,
        out_shape=(
            jax.ShapeDtypeStruct((n_tok, width), BF16),
            jax.ShapeDtypeStruct((2, n_tok), F32),
            shard,
            shard,
            shard,
        ),
        in_specs=[hbm] * 3 + [vmem],
        out_specs=[hbm, vmem] + [hbm] * 3,
        scratch_shapes=[
            pltpu.VMEM((2, chunks, 2 * half, COLS), BF16),
            pltpu.VMEM((2, chunks, half, COLS), BF16),
            pltpu.VMEM((n_tok, width), BF16),
            pltpu.VMEM((2, chunks, 3, half, COLS), F32),
            dma((2, chunks, 2)),
            dma((2, chunks, 3)),
            dma((2,)),
        ],
        compiler_params=pltpu.CompilerParams(vmem_limit_bytes=62 << 20),
        name="widen",
    )(sum_gu, sum_d, d_tokens, d_probs)
    return d_tokens, d_probs.T, grad_g[None], grad_u[None], grad_d[None]


def solution(mesh):
    rows, experts = P(("expert", "dp"), None), P("expert", None, None)
    split = P("expert", "dp", None)
    return jax.shard_map(
        per_device,
        mesh=mesh,
        in_specs=(rows, rows, rows, rows, experts, experts, experts),
        out_specs=(rows, rows, split, split, split),
        check_vma=False,
    )
```

```python
import functools

import jax
import jax.numpy as jnp
from jax import lax
from jax.experimental import pallas as pl
from jax.experimental.pallas import tpu as pltpu
from jax.sharding import PartitionSpec as P

F32 = jnp.float32
BF16 = jnp.bfloat16
MESH = pl.DeviceIdType.MESH
NT = (((1,), (1,)), ((), ()))
TN = (((0,), (0,)), ((), ()))
NN = (((1,), (0,)), ((), ()))

RINGS = (
    ((2, 0), (0, 2), (2, 2)),
    ((2, 1), (1, 2), (2, 3), (3, 2)),
    ((1, 1), (3, 3), (1, 3), (3, 1)),
    ((1, 0), (0, 1), (3, 0), (0, 3)),
)
SHIFTS = [(0, 0, 0), (0, 0, 1)] + [
    (dx, dy, dc) for ring in RINGS for dc in (0, 1) for dx, dy in ring
]
CAP = 32
PROB_ROWS = CAP // 2
GROUP = 8
ROWS = GROUP * CAP
COLS = 512
PIECES = ((0, 0, 512), (1, 0, 512), (2, 0, 512), (3, 0, 256), (3, 256, 256))
HALVES = 8


def dot(a, b, dims):
    return lax.dot_general(a, b, dims, preferred_element_type=F32)


def kernel(
    tok_hbm,
    dy_hbm,
    routes_ref,
    probs_ref,
    wg_hbm,
    wu_hbm,
    wd_hbm,
    dtok_hbm,
    dprob_ref,
    sum_gu_hbm,
    sum_d_hbm,
    tok_ref,
    dy_ref,
    dtok_ref,
    pick,
    pick_scaled,
    xs,
    ss,
    xr,
    sr,
    wgu,
    wd,
    dgu,
    act,
    slope,
    silus,
    backs,
    own_d,
    back_s,
    back_r,
    prob_s,
    prob_r,
    far_gu,
    far_d,
    mid_gu,
    mid_d,
    near_gu,
    near_d,
    w_sem,
    x_s,
    x_r,
    s_s,
    s_r,
    back_ss,
    back_rs,
    prob_ss,
    prob_rs,
    gu_s,
    gu_r,
    d_s,
    d_r,
    sum_sem,
    tok_sem,
    dy_sem,
    dtok_sem,
):
    me, z = lax.axis_index("expert"), lax.axis_index("dp")
    cx, cy, core = me // 8, (me // 2) % 4, me % 2
    up, down, across = (z + 1) % 4, (z + 3) % 4, (z + 2) % 4
    n_shift = len(SHIFTS)
    groups = n_shift // GROUP
    n_tok, width = tok_ref.shape
    chunks = width // COLS
    half = wd.shape[0] // HALVES

    def owner(i):
        dx, dy, dc = SHIFTS[i]
        return ((cx + dx) % 4) * 8 + ((cy + dy) % 4) * 2 + (core + dc) % 2

    def source(i):
        dx, dy, dc = SHIFTS[i]
        return ((cx + 4 - dx) % 4) * 8 + ((cy + 4 - dy) % 4) * 2 + (core + dc) % 2

    def remote(src, dst, send_sem, recv_sem, device):
        return pltpu.make_async_remote_copy(
            src_ref=src,
            dst_ref=dst,
            send_sem=send_sem,
            recv_sem=recv_sem,
            device_id=device,
            device_id_type=MESH,
        )

    barrier = pltpu.get_barrier_semaphore()
    for i in range(1, n_shift):
        pl.semaphore_signal(barrier, inc=1, device_id=(owner(i), z), device_id_type=MESH)
    for other in (up, down):
        pl.semaphore_signal(barrier, inc=1, device_id=(me, other), device_id_type=MESH)

    tok_load = pltpu.make_async_copy(tok_hbm, tok_ref, tok_sem)
    tok_load.start()
    dy_load = pltpu.make_async_copy(dy_hbm, dy_ref, dy_sem)
    loads = [
        pltpu.make_async_copy(wd_hbm, wd, w_sem.at[0]),
    ]
    for h in range(HALVES):
        for j, w in enumerate((wg_hbm, wu_hbm)):
            loads.append(
                pltpu.make_async_copy(
                    w.at[h * half : (h + 1) * half],
                    wgu.at[(2 * h + j) * half : (2 * h + j + 1) * half],
                    w_sem.at[1 + 2 * h + j],
                )
            )

    line = lax.broadcasted_iota(jnp.int32, (128, n_tok), 0)
    routes = routes_ref[...].astype(F32)
    probs = probs_ref[...].astype(F32)
    table = jnp.where(line == 0, routes[0:1], routes[1:2])
    table = jnp.where(line == 2, probs[0:1], table)
    table = jnp.where(line == 3, probs[1:2], table).T
    lane = lax.broadcasted_iota(jnp.int32, (n_tok, 128), 1)
    place = jnp.zeros((1, 128), jnp.int32)
    for i in range(1, n_shift):
        place = place + jnp.where(lane[0:1] == owner(i), i * CAP, 0)
    earlier = (
        lax.broadcasted_iota(jnp.int32, (n_tok, n_tok), 0)
        > lax.broadcasted_iota(jnp.int32, (n_tok, n_tok), 1)
    )
    earlier = jnp.where(earlier, 1.0, 0.0).astype(BF16)
    slot = lax.broadcasted_iota(jnp.int32, (n_tok, ROWS), 1)
    offset = place.astype(F32)
    targets = []
    for k in range(2):
        named = lane == table[:, k : k + 1].astype(jnp.int32)
        hot = jnp.where(named, 1.0, 0.0)
        rank = dot(earlier, hot.astype(BF16), NN) + offset
        offset = offset + jnp.sum(hot, axis=0, keepdims=True)
        target = jnp.sum(jnp.where(named, rank, 0.0), axis=1, keepdims=True)
        targets.append(target.astype(jnp.int32))

    tok_load.wait()
    for g in range(groups):
        at = slice(g * ROWS, (g + 1) * ROWS)
        chosen = [slot == target - g * ROWS for target in targets]
        both = jnp.where(chosen[0] | chosen[1], 1.0, 0.0).astype(BF16)
        for c in range(chunks):
            cols = slice(c * COLS, (c + 1) * COLS)
            xs[c, at] = dot(both, tok_ref[:, cols], TN).astype(BF16)
            if g == 0 and c == 0:
                pl.semaphore_wait(barrier, n_shift + 1)
            for i in range(max(1, g * GROUP), (g + 1) * GROUP):
                rows = slice(i * CAP, (i + 1) * CAP)
                remote(
                    xs.at[c, rows], xr.at[c, rows], x_s, x_r.at[g], (owner(i), z)
                ).start()
        if g == 0:
            for load in [dy_load] + loads:
                load.start()
        scaled = jnp.zeros((n_tok, ROWS), F32)
        for k in range(2):
            pick[k, :, at] = jnp.where(chosen[k], 1.0, 0.0).astype(BF16)
            scaled = scaled + jnp.where(chosen[k], table[:, 2 + k : 3 + k], 0.0)
        pick_scaled[:, at] = scaled.astype(BF16)
    dy_load.wait()
    for c in range(chunks):
        cols = slice(c * COLS, (c + 1) * COLS)
        for g in range(groups):
            at = slice(g * ROWS, (g + 1) * ROWS)
            ss[c, at] = dot(pick_scaled[:, at], dy_ref[:, cols], TN).astype(BF16)
        for j, (block, low, size) in enumerate(PIECES):
            for i in range(1, n_shift) if block == c else ():
                at = (c, slice(i * CAP, (i + 1) * CAP), slice(low, low + size))
                remote(ss.at[at], sr.at[at], s_s, s_r.at[j], (owner(i), z)).start()
    for c in range(chunks):
        xr[c, 0:CAP] = xs[c, 0:CAP]
        sr[c, 0:CAP] = ss[c, 0:CAP]
    for load in loads:
        load.wait()

    for g in range(groups):
        first = CAP if g == 0 else g * ROWS
        took = slice(first, (g + 1) * ROWS)
        remote(xs.at[:, took], xr.at[:, took], x_s, x_r.at[g], (me, z)).wait_recv()
        at = slice(g * ROWS, (g + 1) * ROWS)

        def project(t, _, at=at):
            rows = pl.ds(pl.multiple_of(t * 4 * half, 4 * half), 4 * half)
            pre = jnp.zeros((4 * half, ROWS), F32)
            for c in range(chunks):
                cols = slice(c * COLS, (c + 1) * COLS)
                pre = pre + dot(wgu[rows, cols], xr[c, at], NT)
            for j in range(2):
                gate = pre[2 * j * half : (2 * j + 1) * half]
                upward = pre[(2 * j + 1) * half : (2 * j + 2) * half]
                into = pl.ds(pl.multiple_of((2 * t + j) * half, half), half)
                sig = jax.nn.sigmoid(gate)
                silu = gate * sig
                act[into, at] = (silu * upward).astype(BF16)
                slope[into, at] = upward * (sig + silu * (1.0 - sig))
                silus[into, at] = silu
            return 0

        lax.fori_loop(0, HALVES // 2, project, 0)

    sent = slice(CAP, n_shift * CAP)
    remote(xs.at[:, sent], xr.at[:, sent], x_s, x_r.at[0], (me, z)).wait_send()

    def part_rows(h, size):
        return pl.ds(pl.multiple_of(h * size, size), size)

    def piece(j):
        block, low, size = PIECES[j]
        return block, slice(low, low + size)

    def down_half(h, j):
        block, cols = piece(j)
        return dot(act[part_rows(h, half)], sr[block, :, cols], NN)

    D_ROWS = [slice(k * half, (k + 1) * half) for k in range(6)]

    def down_copy(k, j):
        block, cols = piece(j)
        dst = (far_d.at[0], far_d.at[1], mid_d.at[1], mid_d.at[0], near_d.at[0], near_d.at[1])
        return remote(
            xs.at[block, D_ROWS[k], cols],
            dst[k].at[block, :, cols],
            d_s.at[k, j],
            d_r.at[k, j],
            (me, up if k % 2 == 0 else down),
        )

    halves = (2 * across, 2 * across + 1, 2 * up + 1, 2 * down, 2 * up, 2 * down + 1)

    def down_first(j):
        block, cols = piece(j)
        for k in range(4):
            xs[block, D_ROWS[k], cols] = down_half(halves[k], j).astype(BF16)
            down_copy(k, j).start()
        for part in range(2):
            at = (part * chunks + block) * half
            own_d[at : at + half, cols] = down_half(2 * z + part, j)

    def down_second(j):
        block, cols = piece(j)
        for k in range(4, 6):
            value = down_half(halves[k], j)
            down_copy(k - 4, j).wait_recv()
            value = value + far_d[k - 4, block, :, cols].astype(F32)
            xs[block, D_ROWS[k], cols] = value.astype(BF16)
            down_copy(k, j).start()

    def piece_arrived(j):
        block, cols = piece(j)
        at = (block, sent, cols)
        remote(ss.at[at], sr.at[at], s_s, s_r.at[j], (me, z)).wait_recv()

    def weight_cols(j):
        block, low, size = PIECES[j]
        return slice(block * COLS + low, block * COLS + low + size)

    big = 4 * half
    last = len(PIECES) - 1
    for j in range(last):
        block, cols = piece(j)
        piece_arrived(j)
        down_first(j)

        def project_back(t, _, j=j, block=block, cols=cols):
            rows = part_rows(t, big)
            value = dot(wd[rows, weight_cols(j)], sr[block, :, cols], NT)
            backs[rows] = value if j == 0 else backs[rows] + value
            return 0

        lax.fori_loop(0, HALVES // 4, project_back, 0)
        down_second(j)

    piece_arrived(last)
    remote(ss.at[:, sent], sr.at[:, sent], s_s, s_r.at[0], (me, z)).wait_send()
    last_block, last_cols = piece(last)

    def finish_half(h):
        rows = part_rows(h, half)
        rest = dot(wd[rows, weight_cols(last)], sr[last_block, :, last_cols], NT)
        back = backs[rows] + rest
        dgu[pl.ds(pl.multiple_of(2 * h * half, 2 * half), half)] = (
            back * slope[rows]
        ).astype(BF16)
        dgu[pl.ds(pl.multiple_of((2 * h + 1) * half, half), half)] = (
            back * silus[rows]
        ).astype(BF16)
        return jnp.sum(act[rows].astype(F32) * back, axis=0, keepdims=True)

    def gate_up_half(h, c):
        return dot(dgu[part_rows(h, 2 * half)], xr[c], NN)

    def gate_up_copy(k, c):
        dst = (far_gu.at[0], far_gu.at[1], mid_gu.at[1], mid_gu.at[0], near_gu.at[0], near_gu.at[1])
        size = 2 * half
        if k < 5:
            src = ss.at[c, k * size : (k + 1) * size]
        else:
            src = xs.at[c, 6 * half : 6 * half + size]
        return src, remote(
            src,
            dst[k].at[c],
            gu_s.at[k, c],
            gu_r.at[k, c],
            (me, up if k % 2 == 0 else down),
        )

    def send_gate_up(k, c):
        value = gate_up_half(halves[k], c)
        src, copy = gate_up_copy(k, c)
        if k >= 4:
            gate_up_copy(k - 4, c)[1].wait_recv()
            value = value + far_gu[k - 4, c].astype(F32)
        src[...] = value.astype(BF16)
        copy.start()

    def return_tile(g, n):
        at = slice(g * ROWS, (g + 1) * ROWS)
        cols = pl.ds(pl.multiple_of(n * COLS, COLS), COLS)
        back_s[n, at] = dot(dgu[:, at], wgu[:, cols], TN).astype(BF16)
        for i in range(max(1, g * GROUP), (g + 1) * GROUP):
            rows = slice(i * CAP, (i + 1) * CAP)
            remote(
                back_s.at[n, rows],
                back_r.at[n, rows],
                back_ss,
                back_rs.at[n],
                (source(i), z),
            ).start()

    total = finish_half(halves[0]) + finish_half(halves[1])
    send_gate_up(0, 0)
    send_gate_up(1, 0)
    total = lax.fori_loop(
        2, HALVES, lambda i, t: t + finish_half((2 * across + i) % HALVES), total
    )

    def with_far(n, _):
        @pl.when(n < chunks - 1)
        def _():
            send_gate_up(0, n + 1)
            send_gate_up(1, n + 1)

        return_tile(0, n)
        return 0

    lax.fori_loop(0, chunks, with_far, 0)

    def with_near(n, _):
        send_gate_up(2, n)
        send_gate_up(3, n)
        return_tile(1, n)
        return 0

    lax.fori_loop(0, chunks, with_near, 0)

    high = total.astype(BF16).astype(F32)
    line = lax.broadcasted_iota(jnp.int32, (128, n_shift * CAP), 0)
    upper = lax.broadcasted_iota(jnp.int32, (128, n_shift * CAP), 1) % CAP // PROB_ROWS
    pair = jnp.where(line == 2 * upper, high, 0.0)
    pair = jnp.where(line == 2 * upper + 1, total - high, pair)
    pair = pair.T.reshape(n_shift, 2, PROB_ROWS, 128)
    pair = (pair[:, 0] + pair[:, 1]).astype(BF16)
    prob_s[...] = pair.reshape(n_shift * PROB_ROWS, 128)
    prob_sent = slice(PROB_ROWS, n_shift * PROB_ROWS)
    for i in range(1, n_shift):
        rows = slice(i * PROB_ROWS, (i + 1) * PROB_ROWS)
        remote(
            prob_s.at[rows], prob_r.at[rows], prob_ss, prob_rs, (source(i), z)
        ).start()
    down_first(last)

    def rest_back(n, _):
        return_tile(2, n)
        return_tile(3, n)
        return 0

    lax.fori_loop(0, chunks, rest_back, 0)

    def with_far_sum(c, _):
        send_gate_up(4, c)
        send_gate_up(5, c)
        return 0

    lax.fori_loop(0, chunks, with_far_sum, 0)
    down_second(last)
    for part in range(2):

        def keep(c, _, part=part):
            value = gate_up_half(2 * z + part, c)
            gate_up_copy(3 - part, c)[1].wait_recv()
            value = value + mid_gu[part, c].astype(F32)
            rows = part_rows(part * chunks + c, half)
            slope[rows, 0:COLS] = value[0:half]
            slope[rows, COLS : 2 * COLS] = value[half : 2 * half]
            return 0

        lax.fori_loop(0, chunks, keep, 0)
        for j in range(last + 1):
            down_copy(3 - part, j).wait_recv()
        for c in range(chunks):
            at = slice((part * chunks + c) * half, (part * chunks + c + 1) * half)
            own_d[at] = own_d[at] + mid_d[part, c].astype(F32)
    back_r[:, 0:CAP] = back_s[:, 0:CAP]
    prob_r[0:PROB_ROWS] = prob_s[0:PROB_ROWS]
    remote(
        prob_s.at[prob_sent], prob_r.at[prob_sent], prob_ss, prob_rs, (me, z)
    ).wait_recv()
    terms = prob_r[...].astype(F32).reshape(n_shift, PROB_ROWS, 128)
    column = lax.broadcasted_iota(jnp.int32, terms.shape, 2)
    terms = jnp.stack(
        [jnp.where(column < 2, terms, 0.0), jnp.where(column >= 2, terms, 0.0)], axis=1
    )
    terms = terms.reshape(n_shift * CAP, 128).astype(BF16)
    for k in range(2):
        mine = dot(pick[k], terms, NN).T
        dprob_ref[k : k + 1] = (
            jnp.sum(mine, axis=0, keepdims=True) / probs_ref[...].astype(F32)[k : k + 1]
        )

    def token_copy(n):
        cols = pl.ds(pl.multiple_of(n * COLS, COLS), COLS)
        return pltpu.make_async_copy(dtok_ref.at[n], dtok_hbm.at[:, cols], dtok_sem.at[n])

    def combine(n, _):
        remote(
            back_s.at[n, sent], back_r.at[n, sent], back_ss, back_rs.at[n], (me, z)
        ).wait_recv()
        both = pick[0] + pick[1]
        dtok_ref[n] = dot(both, back_r[n], NN).astype(BF16)
        token_copy(n).start()
        return 0

    def sum_copy(j, part, c):
        src, dst = ((near_gu, sum_gu_hbm), (near_d, sum_d_hbm))[j]
        return pltpu.make_async_copy(
            src.at[part, c], dst.at[part, c], sum_sem.at[j, part, c]
        )

    def complete(c, _):
        for part in range(2):
            gate_up_copy(4 + part, c)[1].wait_recv()
            rows = part_rows(part * chunks + c, half)
            for j in range(2):
                at = slice(j * half, (j + 1) * half)
                value = slope[rows, j * COLS : (j + 1) * COLS]
                near_gu[part, c, at] = (value + near_gu[part, c, at].astype(F32)).astype(BF16)
            sum_copy(0, part, c).start()
        return 0

    def combine_and_complete(c, _):
        combine(c, 0)
        return complete(c, 0)

    lax.fori_loop(0, chunks, combine_and_complete, 0)

    for j in range(last + 1):
        for part in range(2):
            down_copy(4 + part, j).wait_recv()

    def complete_down(c, _):
        for part in range(2):
            value = own_d[part_rows(part * chunks + c, half)]
            near_d[part, c] = (value + near_d[part, c].astype(F32)).astype(BF16)
            sum_copy(1, part, c).start()
        return 0

    lax.fori_loop(0, chunks, complete_down, 0)
    for k in range(6):
        for j in range(last + 1):
            down_copy(k, j).wait_send()

    def finish(c, _):
        token_copy(c).wait()
        for k in range(6):
            gate_up_copy(k, c)[1].wait_send()
        for part in range(2):
            for j in range(2):
                sum_copy(j, part, c).wait()
        return 0

    lax.fori_loop(0, chunks, finish, 0)
    remote(
        back_s.at[:, sent], back_r.at[:, sent], back_ss, back_rs.at[0], (me, z)
    ).wait_send()
    remote(
        prob_s.at[prob_sent], prob_r.at[prob_sent], prob_ss, prob_rs, (me, z)
    ).wait_send()


def widen(
    sum_gu_hbm,
    sum_d_hbm,
    tok_in,
    prob_in,
    tok_out,
    prob_out,
    gg_hbm,
    gu_hbm,
    gd_hbm,
    sum_gu,
    sum_d,
    tok,
    wide,
    in_sem,
    out_sem,
    tok_sem,
):
    parts, chunks, half = sum_d.shape[0:3]
    tiles = [(p, c) for c in range(chunks) for p in range(parts)]
    loads = {}
    for t in tiles:
        loads[t] = [
            pltpu.make_async_copy(sum_gu_hbm.at[t], sum_gu.at[t], in_sem.at[t + (0,)]),
            pltpu.make_async_copy(sum_d_hbm.at[t], sum_d.at[t], in_sem.at[t + (1,)]),
        ]
        for load in loads[t]:
            load.start()
    tok_load = pltpu.make_async_copy(tok_in, tok, tok_sem.at[0])
    tok_load.start()
    prob_out[...] = prob_in[...]
    stores = []
    for p, c in tiles:
        for load in loads[p, c]:
            load.wait()
        wide[p, c, 0] = sum_gu[p, c, 0:half].astype(F32)
        wide[p, c, 1] = sum_gu[p, c, half : 2 * half].astype(F32)
        wide[p, c, 2] = sum_d[p, c].astype(F32)
        low = slice(p * half, (p + 1) * half)
        cols = slice(c * COLS, (c + 1) * COLS)
        for j, out in enumerate((gg_hbm, gu_hbm, gd_hbm)):
            store = pltpu.make_async_copy(
                wide.at[p, c, j], out.at[low, cols], out_sem.at[p, c, j]
            )
            store.start()
            stores.append(store)
    tok_load.wait()
    stores.append(pltpu.make_async_copy(tok, tok_out, tok_sem.at[1]))
    stores[-1].start()
    for store in stores:
        store.wait()


def per_device(tokens, grad_out, routes, gate_probs, w_gate, w_up, w_down):
    n_tok, width = tokens.shape
    hidden = w_gate.shape[1]
    half = hidden // HALVES
    slots = len(SHIFTS) * CAP
    chunks = width // COLS
    vmem = pl.BlockSpec(memory_space=pltpu.VMEM)
    hbm = pl.BlockSpec(memory_space=pl.ANY)
    weights = [w[0] for w in (w_gate, w_up, w_down)]
    dma = pltpu.SemaphoreType.DMA
    d_tokens, d_probs, sum_gu, sum_d = pl.pallas_call(
        kernel,
        out_shape=(
            jax.ShapeDtypeStruct((n_tok, width), BF16),
            jax.ShapeDtypeStruct((2, n_tok), F32),
            jax.ShapeDtypeStruct((2, chunks, 2 * half, COLS), BF16),
            jax.ShapeDtypeStruct((2, chunks, half, COLS), BF16),
        ),
        in_specs=[hbm, hbm, vmem, vmem] + [hbm] * 3,
        out_specs=[hbm, vmem, hbm, hbm],
        scratch_shapes=[
            pltpu.VMEM((n_tok, width), BF16),
            pltpu.VMEM((n_tok, width), BF16),
            pltpu.VMEM((chunks, n_tok, COLS), BF16),
            pltpu.VMEM((2, n_tok, slots), BF16),
            pltpu.VMEM((n_tok, slots), BF16),
            pltpu.VMEM((chunks, slots, COLS), BF16),
            pltpu.VMEM((chunks, slots, COLS), BF16),
            pltpu.VMEM((chunks, slots, COLS), BF16),
            pltpu.VMEM((chunks, slots, COLS), BF16),
            pltpu.VMEM((2 * hidden, width), BF16),
            pltpu.VMEM((hidden, width), BF16),
            pltpu.VMEM((2 * hidden, slots), BF16),
            pltpu.VMEM((hidden, slots), BF16),
            pltpu.VMEM((hidden, slots), F32),
            pltpu.VMEM((hidden, slots), F32),
            pltpu.VMEM((hidden, slots), F32),
            pltpu.VMEM((hidden, COLS), F32),
            pltpu.VMEM((chunks, slots, COLS), BF16),
            pltpu.VMEM((chunks, slots, COLS), BF16),
            pltpu.VMEM((slots // 2, 128), BF16),
            pltpu.VMEM((slots // 2, 128), BF16),
            pltpu.VMEM((2, chunks, 2 * half, COLS), BF16),
            pltpu.VMEM((2, chunks, half, COLS), BF16),
            pltpu.VMEM((2, chunks, 2 * half, COLS), BF16),
            pltpu.VMEM((2, chunks, half, COLS), BF16),
            pltpu.VMEM((2, chunks, 2 * half, COLS), BF16),
            pltpu.VMEM((2, chunks, half, COLS), BF16),
            dma((1 + 2 * HALVES,)),
            dma,
            dma((len(SHIFTS) // GROUP,)),
            dma,
            dma((len(PIECES),)),
            dma,
            dma((chunks,)),
            dma,
            dma,
            dma((6, chunks)),
            dma((6, chunks)),
            dma((6, len(PIECES))),
            dma((6, len(PIECES))),
            dma((2, 2, chunks)),
            dma,
            dma,
            dma((chunks,)),
        ],
        compiler_params=pltpu.CompilerParams(
            collective_id=0, has_side_effects=True, vmem_limit_bytes=63 << 20
        ),
        name="routed_backward",
    )(tokens, grad_out, routes.T, gate_probs.T, *weights)
    shard = jax.ShapeDtypeStruct((hidden // 4, width), F32)
    d_tokens, d_probs, grad_g, grad_u, grad_d = pl.pallas_call(
        widen,
        out_shape=(
            jax.ShapeDtypeStruct((n_tok, width), BF16),
            jax.ShapeDtypeStruct((2, n_tok), F32),
            shard,
            shard,
            shard,
        ),
        in_specs=[hbm] * 3 + [vmem],
        out_specs=[hbm, vmem] + [hbm] * 3,
        scratch_shapes=[
            pltpu.VMEM((2, chunks, 2 * half, COLS), BF16),
            pltpu.VMEM((2, chunks, half, COLS), BF16),
            pltpu.VMEM((n_tok, width), BF16),
            pltpu.VMEM((2, chunks, 3, half, COLS), F32),
            dma((2, chunks, 2)),
            dma((2, chunks, 3)),
            dma((2,)),
        ],
        compiler_params=pltpu.CompilerParams(vmem_limit_bytes=62 << 20),
        name="widen",
    )(sum_gu, sum_d, d_tokens, d_probs)
    return d_tokens, d_probs.T, grad_g[None], grad_u[None], grad_d[None]


def solution(mesh):
    rows, experts = P(("expert", "dp"), None), P("expert", None, None)
    split = P("expert", "dp", None)
    return jax.shard_map(
        per_device,
        mesh=mesh,
        in_specs=(rows, rows, rows, rows, experts, experts, experts),
        out_specs=(rows, rows, split, split, split),
        check_vma=False,
    )
```
